256 devices in a mesh: region: 32 (over x, y, core), batch: 8 (over z).
Axes of the slice: x: 4, y: 4, z: 8, core: 2. Of those that a mesh axis runs over, the one named last changes fastest.
Arguments:
- child_values: int32 [512, 32], P('batch'), may hold values from 0 to 255
- parent_values: int32 [512, 32], P('batch'), may hold values from 0 to 255
- child_logits: bfloat16 [32, 256, 4096], P(None, None, 'region'), may hold values from -254 to 12
- parent_logits: bfloat16 [32, 256, 4096], P(None, None, 'region'), may hold values from -254 to 12
- prior_logits: float32 [32, 4096], P(None, 'region'), may hold values from -8 to 8
- weights: bfloat16 [32, 32, 4, 128, 128], P(None, 'region'), may hold values from 0.049804688 to 1
- block_cols: int32 [32, 32, 4], P(None, 'region'), may hold values from 0 to 31, as said below
- parent_map: int32 [32], replicated, may hold values from 0 to 31
Outputs:
- counts: bfloat16 [32, 32, 4, 128, 128], P(None, 'region', None, 'batch')
- loglik: float32 [512], P('batch')
The draws below stay inside these ranges and needn't reach their ends.
Inputs may be any that keep to these rules, and one draw needn't show every extreme that they name: `block_cols`: the 4 block columns of one block row are different.
All inputs are finite; a program needn't handle non-finite values.
Results may differ from the reference program's by a relative error of at most 0.015.
Values may be sent and summed in bfloat16 or wider, within the bound.
No kernel may reach another device: no remote copies, remote signals or barrier semaphores. Data moves between devices by JAX's collectives and lax.ppermute only.
A program may use at most 128 MiB of HBM per device.

```python
import math
import jax
import jax.numpy as jnp
from jax import lax

K = 4096
CAT = 256
BLK = 128
NZ = 4
C = 32
P_SIZE = 32
NB = 32
S = 512


def draw_child_logits(key, part):
    key = jax.random.fold_in(key, 11)
    noise_key = jax.random.fold_in(key, 0)
    base = jnp.clip(jax.random.normal(noise_key, (C, CAT, K), jnp.float32), -6.0, 6.0)
    return (2.0 * base).astype(jnp.bfloat16)


def draw_parent_logits(key, part):
    key = jax.random.fold_in(key, 12)
    noise_key = jax.random.fold_in(key, 0)
    base = jnp.clip(jax.random.normal(noise_key, (P_SIZE, CAT, K), jnp.float32), -6.0, 6.0)
    return (2.0 * base).astype(jnp.bfloat16)


def pick_columns(row_key):
    return jax.random.permutation(row_key, K // BLK)[:NZ]


def draw_block_cols(key, part):
    key = jax.random.fold_in(key, 13)
    row_keys = jax.random.split(key, C * (K // BLK))
    chosen = jax.vmap(pick_columns)(row_keys)
    return chosen.reshape(C, K // BLK, NZ).astype(jnp.int32)


def set_ends(drawn, stream_key, low, high):
    shape = drawn.shape
    index_at = [jax.random.randint(jax.random.fold_in(stream_key, axis), (), 0, shape[axis]) for axis in range(len(shape))]
    drawn = drawn.at[tuple(index_at)].set(low)
    longest = shape.index(max(shape))
    index_at[longest] = (index_at[longest] + 1) % shape[longest]
    return drawn.at[tuple(index_at)].set(high)


def shard_levels(rng, shape, cuts, least, high):
    gain, own = 1.0, jax.random.fold_in(rng, 6)
    for position, parts in cuts:
        steps = jnp.exp(jax.random.uniform(jax.random.fold_in(own, position), (parts,), jnp.float32, least / len(cuts), high / len(cuts)))
        gain = gain * jnp.repeat(steps, shape[position] // parts).reshape([-1 if axis == position else 1 for axis in range(len(shape))])
    return gain


def bell_draw(key, dims, spread, most, shards=(), kind=jnp.bfloat16):
    result = spread * jax.random.normal(key, dims, jnp.float32)
    if shards:
        result = result * shard_levels(key, dims, shards, -0.22, 0.18)
    return jnp.clip(result, -most, most).astype(kind)


def setup_inputs(seed: int = 0) -> dict:
    keys = jax.random.split(jax.random.key(seed), 9)
    return {
        "child_values": set_ends(jax.random.randint(keys[0], (S, C), 0, CAT), jax.random.fold_in(keys[0], 1), 0, CAT - 1).astype(jnp.int32),
        "parent_values": set_ends(jax.random.randint(keys[1], (S, P_SIZE), 0, CAT), jax.random.fold_in(keys[1], 1), 0, CAT - 1).astype(jnp.int32),
        "child_logits": draw_child_logits(jax.random.fold_in(keys[8], 71), 0),
        "parent_logits": draw_parent_logits(jax.random.fold_in(keys[8], 71), 0),
        "prior_logits": bell_draw(keys[4], (P_SIZE, K), 2.0, 8.0, ((1, 32),), jnp.float32),
        "weights": jnp.clip(jnp.exp(math.log(1.0) - 2.9996462 * jax.random.uniform(keys[5], (C, NB, NZ, BLK, BLK), jnp.float32) ** shard_levels(keys[5], (C, NB, NZ, BLK, BLK), ((1, 32),), -0.2, 0.2)), 0.049804688, 1.0).astype(jnp.bfloat16),
        "block_cols": draw_block_cols(jax.random.fold_in(keys[8], 71), 0),
        "parent_map": set_ends(jax.random.randint(keys[7], (C,), 0, P_SIZE), jax.random.fold_in(keys[7], 1), 0, P_SIZE - 1).astype(jnp.int32),
    }


precise = lax.Precision.HIGHEST


def emission_input(values, logits):
    logit_table = logits.astype(jnp.float32)
    log_norm = jax.nn.logsumexp(logit_table, axis=0)
    one_hot = (values[:, None] == jnp.arange(logits.shape[0], dtype=jnp.int32)[None, :]).astype(jnp.bfloat16)
    return jnp.dot(one_hot, logits, preferred_element_type=jnp.float32) - log_norm[None, :]


def child_pass(values, logits, weights, column_ids):
    inputs = emission_input(values, logits)
    peak_value = jnp.max(inputs, axis=1, keepdims=True)
    scaled = jnp.exp(inputs - peak_value).astype(jnp.bfloat16)
    blocked = scaled.reshape(scaled.shape[0], NB, BLK)
    picked = blocked[:, column_ids].astype(jnp.float32)
    row_sums = jnp.einsum("izrj,sizj->sir", weights.astype(jnp.float32), picked, precision=precise)
    row_sums = row_sums.reshape(scaled.shape[0], K)
    return jnp.log(row_sums) + peak_value, row_sums, picked


def reference(child_values, parent_values, child_logits, parent_logits, prior_logits, weights, block_cols, parent_map):
    def message_of(index):
        message, row_sums, picked = child_pass(child_values[:, index], child_logits[index], weights[index], block_cols[index])
        return message

    indices = jnp.arange(C, dtype=jnp.int32)
    messages = lax.map(message_of, indices)
    incoming = jax.ops.segment_sum(messages, parent_map, num_segments=P_SIZE)
    parent_in = jax.vmap(emission_input, in_axes=(1, 0))(parent_values, parent_logits)
    root_raw = parent_in + incoming + prior_logits[:, None, :]
    root_norm = jax.nn.logsumexp(root_raw, axis=2)
    prior_norm = jax.nn.logsumexp(prior_logits, axis=1)
    loglik = jnp.sum(root_norm - prior_norm[:, None], axis=0) / (C + P_SIZE)
    posterior = jnp.exp(root_raw - root_norm[:, :, None]).astype(jnp.bfloat16)
    factor = K * NZ * BLK / S

    def counts_of(index):
        message, row_sums, picked = child_pass(child_values[:, index], child_logits[index], weights[index], block_cols[index])
        share_rows = (posterior[parent_map[index]].astype(jnp.float32) / row_sums).astype(jnp.bfloat16)
        share_rows = share_rows.astype(jnp.float32).reshape(-1, NB, BLK)
        flow_block = jnp.einsum("sir,sizj->izrj", share_rows, picked, precision=precise)
        return (flow_block * weights[index].astype(jnp.float32) * factor).astype(jnp.bfloat16)

    counts = lax.map(counts_of, indices)
    return counts, loglik
```

```python
import jax
import jax.numpy as jnp
from jax import lax
from jax.experimental import pallas as pl
from jax.experimental.pallas import tpu as pltpu
from jax.sharding import PartitionSpec as P

K = 4096
BLK = 128
NZ = 4
C = 32
P_SIZE = 32
S_LOC = 64
LN2 = 0.6931471805599453
LOG2E = 1.4426950408889634
GROUP = 8
VMEM = pl.BlockSpec(memory_space=pltpu.VMEM)
SMEM = pl.BlockSpec(memory_space=pltpu.SMEM)
ANY = pl.BlockSpec(memory_space=pl.ANY)


def lane_of(shape):
    return lax.broadcasted_iota(jnp.int32, shape, len(shape) - 1)


def look_up(values, table_ref, index):
    table = table_ref[index]
    wide = table.astype(jnp.float32)
    top = jnp.max(wide, axis=0, keepdims=True)
    log_norm = jnp.log(jnp.sum(jnp.exp(wide - top), axis=0, keepdims=True)) + top
    hot = (values[:, index : index + 1] == lane_of((S_LOC, table.shape[0]))).astype(jnp.float32)
    looked = jnp.dot(hot.astype(jnp.bfloat16), table, preferred_element_type=jnp.float32)
    return looked - log_norm


def child_kernel(values_ref, table_ref, out_ref):
    values = values_ref[...]
    powers = jnp.zeros((S_LOC, BLK), jnp.float32)
    lanes = lane_of((S_LOC, BLK))
    for c in range(C):
        inputs = look_up(values, table_ref, c)
        power = jnp.ceil(jnp.max(inputs, axis=1, keepdims=True) * LOG2E)
        power = power.astype(jnp.bfloat16).astype(jnp.float32)
        out_ref[c] = jnp.exp(inputs - power * LN2).astype(jnp.bfloat16)
        powers = jnp.where(lanes == c, power, powers)
    out_ref[C] = powers.astype(jnp.bfloat16)


def parent_kernel(values_ref, table_ref, prior_ref, out_ref):
    values = values_ref[...]
    for p in range(P_SIZE):
        out_ref[p] = look_up(values, table_ref, p) + prior_ref[p : p + 1, :]


def sums_kernel(
    cols_ref, map_ref, gathered_ref, weights_ref, parent_ref, prior_ref,
    stats_ref, root_ref, sums_ref, picked_ref,
    slots, powers, slot_sem, power_sem,
):
    for g in range(C // GROUP):
        def fetch(k, carry, g=g):
            c = g * GROUP + k // NZ
            z = k % NZ
            source = cols_ref[c, z] * (C + 1) + c
            pltpu.make_async_copy(
                gathered_ref.at[source], slots.at[c, z], slot_sem.at[g]
            ).start()
            return carry

        if g == 0:
            def fetch_power(r, carry):
                pltpu.make_async_copy(
                    gathered_ref.at[r * (C + 1) + C], powers.at[r], power_sem
                ).start()
                return carry

            lax.fori_loop(0, powers.shape[0], fetch_power, 0)
        lax.fori_loop(0, GROUP * NZ, fetch, 0)
    root_ref[...] = parent_ref[...]
    pltpu.make_async_copy(powers, powers, power_sem).wait()
    for g in range(C // GROUP):
        part = slots.at[pl.ds(g * GROUP, GROUP)]
        pltpu.make_async_copy(part, part, slot_sem.at[g]).wait()
        for c in range(g * GROUP, (g + 1) * GROUP):
            power = [powers[cols_ref[c, z]].astype(jnp.float32)[:, c : c + 1] for z in range(NZ)]
            top = jnp.maximum(jnp.maximum(power[0], power[1]), jnp.maximum(power[2], power[3]))
            row_sums = None
            for z in range(NZ):
                factor = jnp.broadcast_to(jnp.exp2(power[z] - top), (S_LOC, BLK))
                block = (slots[c, z].astype(jnp.float32) * factor).astype(jnp.bfloat16)
                picked_ref[c, :, z * BLK : (z + 1) * BLK] = block
                term = lax.dot_general(
                    block, weights_ref[c, z], (((1,), (1,)), ((), ())),
                    preferred_element_type=jnp.float32,
                )
                row_sums = term if row_sums is None else row_sums + term
            sums_ref[c] = row_sums
            owner = map_ref[c]
            root_ref[owner] = root_ref[owner] + (jnp.log(row_sums) + top * LN2)
    lanes = lane_of((S_LOC, BLK))
    prior = prior_ref[...]
    prior_peak = jnp.max(prior, axis=1, keepdims=True)
    prior_total = jnp.sum(jnp.exp(prior - prior_peak), axis=1, keepdims=True)
    eye = lax.broadcasted_iota(jnp.int32, (P_SIZE, BLK), 0)
    wide = lane_of((P_SIZE, BLK))
    stats = jnp.sum(
        jnp.where(wide == eye + 2 * P_SIZE, prior_peak, 0.0)
        + jnp.where(wide == eye + 3 * P_SIZE, prior_total, 0.0),
        axis=0, keepdims=True,
    )
    stats = jnp.broadcast_to(stats, (S_LOC, BLK))
    for p in range(P_SIZE):
        root = root_ref[p]
        peak = jnp.max(root, axis=1, keepdims=True)
        total = jnp.sum(jnp.exp(root - peak), axis=1, keepdims=True)
        stats = jnp.where(lanes == p, peak, stats)
        stats = jnp.where(lanes == P_SIZE + p, total, stats)
    stats_ref[...] = stats


def merge(stats):
    is_peak = lane_of((S_LOC, BLK)) % (2 * P_SIZE) < P_SIZE
    peaks = [jnp.where(is_peak, s, pltpu.roll(s, P_SIZE, 1)) for s in stats]
    best = peaks[0]
    for p in peaks[1:]:
        best = jnp.maximum(best, p)
    total = None
    for s, p in zip(stats, peaks):
        term = s * jnp.exp(p - best)
        total = term if total is None else total + term
    return jnp.where(is_peak, best, total)


def merge_kernel(*refs):
    refs[-1][...] = merge([r[...] for r in refs[:-1]])


def counts_kernel(scale, n_stats, map_ref, *refs):
    stats_refs = refs[:n_stats]
    root_ref, sums_ref, picked_ref, weights_ref, out_ref, loglik_ref, posterior = refs[n_stats:]
    stats = merge([r[...] for r in stats_refs])
    lanes = lane_of((S_LOC, BLK))
    norm = stats + pltpu.roll(jnp.log(stats), BLK - P_SIZE, 1)
    signed = jnp.where(lanes < P_SIZE, norm, 0.0) - jnp.where(
        (lanes >= 2 * P_SIZE) & (lanes < 3 * P_SIZE), norm, 0.0
    )
    loglik = jnp.sum(signed, axis=1, keepdims=True) / (C + P_SIZE)
    loglik_ref[...] = jnp.broadcast_to(loglik, (S_LOC, BLK))
    for p in range(P_SIZE):
        posterior[p] = jnp.exp(root_ref[p] - norm[:, p : p + 1]).astype(jnp.bfloat16)
    parts, _, _, rows, _ = out_ref.shape
    for c in range(C):
        share = (posterior[map_ref[c]].astype(jnp.float32) / sums_ref[c]).astype(jnp.bfloat16)
        flow = lax.dot_general(
            share, picked_ref[c], (((0,), (0,)), ((), ())), preferred_element_type=jnp.float32
        )
        for z in range(NZ):
            block = flow[:, z * BLK : (z + 1) * BLK] * (weights_ref[c, z].astype(jnp.float32) * scale)
            out_ref[:, c, z] = block.astype(jnp.bfloat16).reshape(parts, rows, BLK)


def params(mib):
    return pltpu.CompilerParams(vmem_limit_bytes=mib << 20)


def cost(flops, moved, transcendentals):
    return pl.CostEstimate(flops=flops, bytes_accessed=moved, transcendentals=transcendentals)


def along(axis, step):
    pairs = []
    for i in range(32):
        x, y, core = i // 8, i // 2 % 4, i % 2
        if axis == "x":
            x = (x + step) % 4
        elif axis == "y":
            y = (y + step) % 4
        else:
            core = (core + step) % 2
        pairs.append((i, x * 8 + y * 2 + core))
    return pairs


def body(
    child_values,
    parent_values,
    child_logits,
    parent_logits,
    prior_logits,
    weights,
    block_cols,
    parent_map,
):
    f32, bf16 = jnp.float32, jnp.bfloat16
    shape = jax.ShapeDtypeStruct
    devices = lax.axis_size("region")
    parts = lax.axis_size("batch")
    weights = weights[:, 0]
    scaled = pl.pallas_call(
        child_kernel,
        out_shape=shape((C + 1, S_LOC, BLK), bf16),
        in_specs=[VMEM, VMEM],
        out_specs=VMEM,
        compiler_params=params(16),
        cost_estimate=cost(1 << 28, 3 << 20, 1 << 21),
        name="child_scores",
    )(child_values, child_logits)
    gathered = lax.all_gather(scaled.reshape(-1, BLK), "region")
    parent_in = pl.pallas_call(
        parent_kernel,
        out_shape=shape((P_SIZE, S_LOC, BLK), f32),
        in_specs=[VMEM, VMEM, VMEM],
        out_specs=VMEM,
        compiler_params=params(16),
        cost_estimate=cost(1 << 28, 3 << 20, 1 << 21),
        name="parent_scores",
    )(parent_values, parent_logits, prior_logits)
    stats, root, sums, picked = pl.pallas_call(
        sums_kernel,
        out_shape=(
            shape((S_LOC, BLK), f32),
            shape((P_SIZE, S_LOC, BLK), f32),
            shape((C, S_LOC, BLK), f32),
            shape((C, S_LOC, NZ * BLK), bf16),
        ),
        in_specs=[SMEM, SMEM, ANY, VMEM, VMEM, VMEM],
        out_specs=(VMEM,) * 4,
        scratch_shapes=[
            pltpu.VMEM((C, NZ, S_LOC, BLK), bf16),
            pltpu.VMEM((devices, S_LOC, BLK), bf16),
            pltpu.SemaphoreType.DMA((C // GROUP,)),
            pltpu.SemaphoreType.DMA,
        ],
        compiler_params=params(24),
        cost_estimate=cost(1 << 29, 12 << 20, 1 << 20),
        name="row_sums",
    )(
        block_cols[:, 0],
        parent_map,
        gathered.reshape(-1, S_LOC, BLK),
        weights,
        parent_in,
        prior_logits,
    )

    def send(axis, step):
        return lax.ppermute(stats, "region", along(axis, step))

    for axis, steps in (("core", (1,)), ("x", (1, 3, 2))):
        others = [send(axis, step) for step in steps]
        stats = pl.pallas_call(
            merge_kernel,
            out_shape=shape((S_LOC, BLK), f32),
            in_specs=[VMEM] * (1 + len(others)),
            out_specs=VMEM,
            compiler_params=params(4),
            name="merge_" + axis,
        )(stats, *others)
    others = [send("y", step) for step in (1, 3, 2)]
    scale = K * NZ * BLK / (S_LOC * parts)
    flows, loglik = pl.pallas_call(
        lambda *refs: counts_kernel(scale, 1 + len(others), *refs),
        out_shape=(shape((parts, C, NZ, BLK // parts, BLK), bf16), shape((S_LOC, BLK), f32)),
        in_specs=[SMEM] + [VMEM] * (5 + len(others)),
        out_specs=(VMEM, VMEM),
        scratch_shapes=[pltpu.VMEM((P_SIZE, S_LOC, BLK), bf16)],
        compiler_params=params(24),
        cost_estimate=cost(1 << 29, 13 << 20, 1 << 19),
        name="counts",
    )(parent_map, stats, *others, root, sums, picked, weights)
    flows = lax.psum_scatter(flows.reshape(parts, -1, BLK), "batch")
    return (flows.reshape(C, 1, NZ, BLK // parts, BLK), loglik[:, 0])


def solution(mesh):
    return jax.shard_map(
        body,
        mesh=mesh,
        in_specs=(
            P("batch", None),
            P("batch", None),
            P(None, None, "region"),
            P(None, None, "region"),
            P(None, "region"),
            P(None, "region", None, None, None),
            P(None, "region", None),
            P(),
        ),
        out_specs=(P(None, "region", None, "batch", None), P("batch")),
        check_vma=False,
    )
```

```python
import jax
import jax.numpy as jnp
from jax import lax
from jax.experimental import pallas as pl
from jax.experimental.pallas import tpu as pltpu
from jax.sharding import PartitionSpec as P

K = 4096
BLK = 128
NZ = 4
C = 32
P_SIZE = 32
S_LOC = 64
LN2 = 0.6931471805599453
LOG2E = 1.4426950408889634
HALF = C // 2
PIECE = 2 * HALF + 1
VMEM = pl.BlockSpec(memory_space=pltpu.VMEM)
SMEM = pl.BlockSpec(memory_space=pltpu.SMEM)
ANY = pl.BlockSpec(memory_space=pl.ANY)


def lane_of(shape):
    return lax.broadcasted_iota(jnp.int32, shape, len(shape) - 1)


def look_up(values, table):
    wide = table.astype(jnp.float32)
    top = jnp.max(wide, axis=0, keepdims=True)
    log_norm = jnp.log(jnp.sum(jnp.exp(wide - top), axis=0, keepdims=True)) + top
    hot = (values == lane_of((S_LOC, table.shape[0]))).astype(jnp.float32)
    looked = jnp.dot(hot.astype(jnp.bfloat16), table, preferred_element_type=jnp.float32)
    return looked - log_norm


def child_kernel(half_ref, values_ref, table_ref, out_ref, inputs):
    half = half_ref[0]
    values = values_ref[...]
    values = jnp.where(half == 0, values[:, :HALF], values[:, HALF:])
    for k in range(HALF):
        inputs[k] = look_up(values[:, k : k + 1], table_ref[half * HALF + k])
    powers = jnp.zeros((S_LOC, BLK), jnp.float32)
    lanes = lane_of((S_LOC, BLK))
    for k in range(HALF):
        powers = jnp.where(lanes == k, jnp.max(inputs[k], axis=1, keepdims=True), powers)
    powers = jnp.ceil(powers * LOG2E).astype(jnp.bfloat16)
    out_ref[HALF] = powers
    powers = powers.astype(jnp.float32) * LN2
    for k in range(HALF):
        out_ref[k] = jnp.exp(inputs[k] - powers[:, k : k + 1]).astype(jnp.bfloat16)


def pack_kernel(core_ref, own_ref, other_ref, out_ref):
    core = core_ref[0]
    out_ref[pl.ds(core * HALF, HALF)] = own_ref[:HALF]
    out_ref[pl.ds((1 - core) * HALF, HALF)] = other_ref[:HALF]
    own = own_ref[HALF].astype(jnp.float32)
    other = other_ref[HALF].astype(jnp.float32)
    low = jnp.where(core == 0, own, other)
    high = jnp.where(core == 0, other, own)
    powers = jnp.where(lane_of((S_LOC, BLK)) < HALF, low, pltpu.roll(high, HALF, 1))
    out_ref[2 * HALF] = powers.astype(jnp.bfloat16)


def parent_kernel(values_ref, table_ref, prior_ref, out_ref):
    values = values_ref[...]
    for p in range(P_SIZE):
        out_ref[p] = look_up(values[:, p : p + 1], table_ref[p]) + prior_ref[p : p + 1, :]


PLACES = (
    ((0, 0),),
    ((3, 0), (1, 0), (2, 0)),
    ((0, 3),),
    ((0, 1),),
    ((3, 3), (1, 3), (2, 3)),
    ((3, 1), (1, 1), (2, 1)),
    ((3, 2), (1, 2)),
    ((0, 2), (2, 2)),
)


def pick_kernel(code_ref, *refs):
    sources = refs[: len(PLACES)]
    out_refs, pool, powers = refs[len(PLACES) : -2], refs[-2], refs[-1]

    def collect(k, carry):
        for source, places in zip(sources, PLACES):
            for n, (a, b) in enumerate(places):
                pool[(a * 4 + b) * PIECE + k] = source[n * PIECE + k]
        return carry

    lax.fori_loop(0, PIECE, collect, 0)
    for piece in range(16):
        both = pool[piece * PIECE + 2 * HALF].astype(jnp.float32)
        powers[2 * piece] = both
        powers[2 * piece + 1] = pltpu.roll(both, BLK - HALF, 1)
    lanes = lane_of((S_LOC, BLK))
    tops = [jnp.zeros((S_LOC, BLK), jnp.float32)] * 2
    for k in range(HALF):
        for row, out_ref in enumerate(out_refs):
            codes = [code_ref[row * C * NZ // 2 + k * NZ + z] for z in range(NZ)]
            power = [powers[code][:, k : k + 1] for code in codes]
            top = jnp.maximum(jnp.maximum(power[0], power[1]), jnp.maximum(power[2], power[3]))
            tops[row] = jnp.where(lanes == k, top, tops[row])
            for z in range(NZ):
                code = codes[z]
                factor = jnp.broadcast_to(jnp.exp2(power[z] - top), (S_LOC, BLK))
                block = pool[(code // 2) * PIECE + (code % 2) * HALF + k]
                out_ref[k * NZ + z] = (block.astype(jnp.float32) * factor).astype(jnp.bfloat16)
    for row, out_ref in enumerate(out_refs):
        out_ref[HALF * NZ] = tops[row].astype(jnp.bfloat16)


def child_at(core, half, k):
    return jnp.where(core == half, k, HALF + k)


def sums_kernel(
    core_ref, map_ref, own_ref, other_ref, weights_ref, parent_ref, prior_ref,
    stats_ref, root_ref, sums_ref,
):
    core = core_ref[0]
    root_ref[...] = parent_ref[...]
    for half, picked_ref in enumerate((own_ref, other_ref)):
        tops = picked_ref[HALF * NZ].astype(jnp.float32) * LN2
        for k in range(HALF):
            child = child_at(core, half, k)
            row_sums = None
            for z in range(0, NZ, 2):
                picked = jnp.concatenate([picked_ref[k * NZ + z], picked_ref[k * NZ + z + 1]], axis=1)
                wide = jnp.concatenate([weights_ref[child, z], weights_ref[child, z + 1]], axis=1)
                term = lax.dot_general(
                    picked, wide, (((1,), (1,)), ((), ())), preferred_element_type=jnp.float32
                )
                row_sums = term if row_sums is None else row_sums + term
            sums_ref[half * HALF + k] = row_sums
    for half, picked_ref in enumerate((own_ref, other_ref)):
        tops = picked_ref[HALF * NZ].astype(jnp.float32) * LN2
        for k in range(HALF):
            owner = map_ref[child_at(core, half, k)]
            message = jnp.log(sums_ref[half * HALF + k]) + tops[:, k : k + 1]
            root_ref[owner] = root_ref[owner] + message
    lanes = lane_of((S_LOC, BLK))
    prior = prior_ref[...]
    prior_peak = jnp.max(prior, axis=1, keepdims=True)
    prior_total = jnp.sum(jnp.exp(prior - prior_peak), axis=1, keepdims=True)
    eye = lax.broadcasted_iota(jnp.int32, (P_SIZE, BLK), 0)
    wide = lane_of((P_SIZE, BLK))
    stats = jnp.sum(
        jnp.where(wide == eye + 2 * P_SIZE, prior_peak, 0.0)
        + jnp.where(wide == eye + 3 * P_SIZE, prior_total, 0.0),
        axis=0, keepdims=True,
    )
    stats = jnp.broadcast_to(stats, (S_LOC, BLK))
    for p in range(P_SIZE):
        stats = jnp.where(lanes == p, jnp.max(root_ref[p], axis=1, keepdims=True), stats)
    peaks = stats
    for p in range(P_SIZE):
        total = jnp.sum(jnp.exp(root_ref[p] - peaks[:, p : p + 1]), axis=1, keepdims=True)
        stats = jnp.where(lanes == P_SIZE + p, total, stats)
    stats_ref[...] = stats


def merge(stats):
    is_peak = lane_of((S_LOC, BLK)) % (2 * P_SIZE) < P_SIZE
    peaks = [jnp.where(is_peak, s, pltpu.roll(s, P_SIZE, 1)) for s in stats]
    best = peaks[0]
    for p in peaks[1:]:
        best = jnp.maximum(best, p)
    total = None
    for s, p in zip(stats, peaks):
        term = s * jnp.exp(p - best)
        total = term if total is None else total + term
    return jnp.where(is_peak, best, total)


def merge_kernel(*refs):
    refs[-1][...] = merge([r[...] for r in refs[:-1]])


def counts_kernel(scale, n_stats, place_ref, map_ref, *refs):
    stats_refs, refs = refs[:n_stats], refs[n_stats:]
    root_ref, sums_ref, own_ref, other_ref, weights_ref = refs[:5]
    near, far, loglik_ref, posterior = refs[5:12], refs[12:14], refs[14], refs[15]
    core, place = place_ref[0], place_ref[1]
    stats = merge([r[...] for r in stats_refs])
    lanes = lane_of((S_LOC, BLK))
    norm = stats + pltpu.roll(jnp.log(stats), BLK - P_SIZE, 1)
    signed = jnp.where(lanes < P_SIZE, norm, 0.0) - jnp.where(
        (lanes >= 2 * P_SIZE) & (lanes < 3 * P_SIZE), norm, 0.0
    )
    loglik = jnp.sum(signed, axis=1, keepdims=True) / (C + P_SIZE)
    loglik_ref[...] = jnp.broadcast_to(loglik, (S_LOC, BLK))
    for p in range(P_SIZE):
        posterior[p] = jnp.exp(root_ref[p] - norm[:, p : p + 1]).astype(jnp.bfloat16)
    rows = near[0].shape[2]
    parts = BLK // rows
    starts = [pl.multiple_of(lax.rem(place + k, parts) * rows, rows) for k in range(parts)]
    turn = lax.rem(parts - place, parts) * rows
    for half, picked_ref in enumerate((own_ref, other_ref)):
        for k in range(HALF):
            child = child_at(core, half, k)
            share = posterior[map_ref[child]].astype(jnp.float32) / sums_ref[half * HALF + k]
            share = pltpu.roll(share, turn, 1).astype(jnp.bfloat16)
            picked = jnp.concatenate([picked_ref[k * NZ + z] for z in range(NZ)], axis=1)
            flow = lax.dot_general(
                share, picked, (((0,), (0,)), ((), ())), preferred_element_type=jnp.float32
            )
            for distance in range(parts):
                for z in range(NZ):
                    weight = weights_ref[child, z, pl.ds(starts[distance], rows), :]
                    block = flow[distance * rows : (distance + 1) * rows, z * BLK : (z + 1) * BLK]
                    block = (block * (weight.astype(jnp.float32) * scale)).astype(jnp.bfloat16)
                    if distance == 4:
                        far[half][k, z] = block
                    else:
                        near[distance if distance < 4 else distance - 1][half * HALF + k, z] = block


def first_step_kernel(up_ref, down_ref, up_in_ref, down_in_ref, up_out_ref, down_out_ref):
    f32 = jnp.float32
    low, high = pl.ds(0, HALF), pl.ds(HALF, HALF)
    up_out_ref[low] = (up_ref[low].astype(f32) + up_in_ref[...].astype(f32)).astype(jnp.bfloat16)
    up_out_ref[high] = up_ref[high]
    down_out_ref[low] = down_ref[low]
    down_out_ref[high] = (down_ref[high].astype(f32) + down_in_ref[...].astype(f32)).astype(
        jnp.bfloat16
    )


def step_kernel(up_ref, down_ref, up_in_ref, down_in_ref, up_out_ref, down_out_ref):
    f32 = jnp.float32
    up_out_ref[...] = (up_ref[...].astype(f32) + up_in_ref[...].astype(f32)).astype(jnp.bfloat16)
    down_out_ref[...] = (down_ref[...].astype(f32) + down_in_ref[...].astype(f32)).astype(
        jnp.bfloat16
    )


def last_kernel(core_ref, own_ref, up_in_ref, down_in_ref, out_ref):
    f32 = jnp.float32
    core = core_ref[0]
    for half in range(2):
        part = pl.ds(half * HALF, HALF)
        total = own_ref[part].astype(f32) + up_in_ref[part].astype(f32) + down_in_ref[part].astype(f32)
        out_ref[pl.ds(jnp.where(core == half, 0, HALF), HALF)] = total.astype(jnp.bfloat16)


def params(mib):
    return pltpu.CompilerParams(vmem_limit_bytes=mib << 20)


def cost(flops, moved, transcendentals):
    return pl.CostEstimate(flops=flops, bytes_accessed=moved, transcendentals=transcendentals)


def along(a, b):
    pairs = []
    for i in range(32):
        x, y, core = i // 8, i // 2 % 4, i % 2
        dx, dy = (a, b) if core == 0 else (b, a)
        pairs.append((i, (x + dx) % 4 * 8 + (y + dy) % 4 * 2 + core))
    return pairs


SWAP = [(i, i ^ 1) for i in range(32)]


def body(
    child_values,
    parent_values,
    child_logits,
    parent_logits,
    prior_logits,
    weights,
    block_cols,
    parent_map,
):
    f32, bf16, i32 = jnp.float32, jnp.bfloat16, jnp.int32
    shape = jax.ShapeDtypeStruct
    parts = lax.axis_size("batch")
    rows = BLK // parts
    weights = weights[:, 0]
    region = lax.axis_index("region").astype(i32)
    core = lax.rem(region, 2)
    place = jnp.stack([core, lax.axis_index("batch").astype(i32)])

    def scores(half):
        return pl.pallas_call(
            child_kernel,
            out_shape=shape((HALF + 1, S_LOC, BLK), bf16),
            in_specs=[SMEM, VMEM, VMEM],
            out_specs=VMEM,
            scratch_shapes=[pltpu.VMEM((HALF, S_LOC, BLK), f32)],
            compiler_params=params(16),
            cost_estimate=cost(1 << 27, 2 << 20, 1 << 20),
            name="child_scores",
        )(half.reshape(1), child_values, child_logits)

    given = lax.ppermute(scores(1 - core), "region", SWAP)
    kept = scores(core)
    own = pl.pallas_call(
        pack_kernel,
        out_shape=shape((PIECE, S_LOC, BLK), bf16),
        in_specs=[SMEM, VMEM, VMEM],
        out_specs=VMEM,
        compiler_params=params(8),
        name="pack",
    )(place, kept, given)

    def send(value, a, b):
        return lax.ppermute(value, "region", along(a, b))

    a1, a3, a2, b1, b3 = lax.optimization_barrier(
        (send(own, 1, 0), send(own, -1, 0), send(own, 2, 0), send(own, 0, 1), send(own, 0, -1))
    )
    line = jnp.concatenate([a1, a3, a2])
    q1, q3 = send(line, 0, 1), send(line, 0, -1)
    t1 = send(q1[: 2 * PIECE], 0, 1)
    t3 = send(jnp.concatenate([b3, q3[2 * PIECE :]]), 0, -1)

    parent_in = pl.pallas_call(
        parent_kernel,
        out_shape=shape((P_SIZE, S_LOC, BLK), f32),
        in_specs=[VMEM, VMEM, VMEM],
        out_specs=VMEM,
        compiler_params=params(16),
        cost_estimate=cost(1 << 28, 3 << 20, 1 << 21),
        name="parent_scores",
    )(parent_values, parent_logits, prior_logits)

    columns = block_cols[:, 0]
    columns = jnp.stack([columns, lax.ppermute(columns, "region", SWAP)])
    columns = lax.dynamic_slice_in_dim(columns, core * HALF, HALF, axis=1).reshape(-1)
    x, y = columns // 8 - region // 8 + 4, columns // 2 % 4 - region // 2 % 4 + 4
    x, y = x % 4, y % 4
    code = jnp.where(core == 0, x * 4 + y, y * 4 + x) * 2 + columns % 2
    picked, for_other = pl.pallas_call(
        pick_kernel,
        out_shape=(shape((HALF * NZ + 1, S_LOC, BLK), bf16),) * 2,
        in_specs=[SMEM] + [VMEM] * len(PLACES),
        out_specs=(VMEM, VMEM),
        scratch_shapes=[
            pltpu.VMEM((16 * PIECE, S_LOC, BLK), bf16),
            pltpu.VMEM((32, S_LOC, BLK), f32),
        ],
        compiler_params=params(32),
        cost_estimate=cost(1 << 22, 20 << 20, 1 << 20),
        name="pick",
    )(code, own, line, b1, b3, q1, q3, t1, t3)
    other = lax.ppermute(for_other, "region", SWAP)
    stats, root, sums = pl.pallas_call(
        sums_kernel,
        out_shape=(
            shape((S_LOC, BLK), f32),
            shape((P_SIZE, S_LOC, BLK), f32),
            shape((C, S_LOC, BLK), f32),
        ),
        in_specs=[SMEM, SMEM] + [VMEM] * 5,
        out_specs=(VMEM,) * 3,
        compiler_params=params(16),
        cost_estimate=cost(1 << 29, 12 << 20, 1 << 20),
        name="row_sums",
    )(place, parent_map, picked, other, weights, parent_in, prior_logits)

    for axis, pairs in (
        ("core", (SWAP,)),
        ("a", tuple(along(step, 0) for step in (1, 3, 2))),
        ("b", tuple(along(0, step) for step in (1, 3, 2))),
    ):
        others = [lax.ppermute(stats, "region", p) for p in pairs]
        if axis == "b":
            break
        stats = pl.pallas_call(
            merge_kernel,
            out_shape=shape((S_LOC, BLK), f32),
            in_specs=[VMEM] * (1 + len(others)),
            out_specs=VMEM,
            compiler_params=params(4),
            name="merge_" + axis,
        )(stats, *others)
    scale = K * NZ * BLK / (S_LOC * parts)
    whole, half_set = shape((C, NZ, rows, BLK), bf16), shape((HALF, NZ, rows, BLK), bf16)
    n0, n1, n2, n3, n5, n6, n7, far_up, far_down, loglik = pl.pallas_call(
        lambda *refs: counts_kernel(scale, 1 + len(others), *refs),
        out_shape=(whole,) * 7 + (half_set,) * 2 + (shape((S_LOC, BLK), f32),),
        in_specs=[SMEM, SMEM] + [VMEM] * (6 + len(others)),
        out_specs=(VMEM,) * 10,
        scratch_shapes=[pltpu.VMEM((P_SIZE, S_LOC, BLK), bf16)],
        compiler_params=params(24),
        cost_estimate=cost(1 << 29, 13 << 20, 1 << 19),
        name="counts",
    )(place, parent_map, stats, *others, root, sums, picked, other, weights)

    def ring(up, down):
        shift = lambda step: [(i, (i + step) % parts) for i in range(parts)]
        return lax.ppermute(up, "batch", shift(1)), lax.ppermute(down, "batch", shift(-1))

    up, down = ring(far_up, far_down)
    for kernel, here_up, here_down in (
        (first_step_kernel, n3, n5),
        (step_kernel, n2, n6),
        (step_kernel, n1, n7),
    ):
        up, down = ring(
            *pl.pallas_call(
                kernel,
                out_shape=(whole, whole),
                in_specs=[VMEM] * 4,
                out_specs=(VMEM, VMEM),
                compiler_params=params(8),
                name="ring_add",
            )(here_up, here_down, up, down)
        )
    counts = pl.pallas_call(
        last_kernel,
        out_shape=whole,
        in_specs=[SMEM] + [VMEM] * 3,
        out_specs=VMEM,
        compiler_params=params(8),
        name="ring_last",
    )(place, n0, up, down)
    return (counts[:, None], loglik[:, 0])


def solution(mesh):
    return jax.shard_map(
        body,
        mesh=mesh,
        in_specs=(
            P("batch", None),
            P("batch", None),
            P(None, None, "region"),
            P(None, None, "region"),
            P(None, "region"),
            P(None, "region", None, None, None),
            P(None, "region", None),
            P(),
        ),
        out_specs=(P(None, "region", None, "batch", None), P("batch")),
        check_vma=False,
    )
```

```python
import jax
import jax.numpy as jnp
from jax import lax
from jax.experimental import pallas as pl
from jax.experimental.pallas import tpu as pltpu
from jax.sharding import PartitionSpec as P

K = 4096
BLK = 128
NZ = 4
C = 32
P_SIZE = 32
S_LOC = 64
LN2 = 0.6931471805599453
LOG2E = 1.4426950408889634
HALF = C // 2
PIECE = 2 * HALF + 1
VMEM = pl.BlockSpec(memory_space=pltpu.VMEM)
SMEM = pl.BlockSpec(memory_space=pltpu.SMEM)
ANY = pl.BlockSpec(memory_space=pl.ANY)


def lane_of(shape):
    return lax.broadcasted_iota(jnp.int32, shape, len(shape) - 1)


def look_up(values, table):
    wide = table.astype(jnp.float32)
    top = jnp.max(wide, axis=0, keepdims=True)
    log_norm = jnp.log(jnp.sum(jnp.exp(wide - top), axis=0, keepdims=True)) + top
    hot = (values == lane_of((S_LOC, table.shape[0]))).astype(jnp.float32)
    looked = jnp.dot(hot.astype(jnp.bfloat16), table, preferred_element_type=jnp.float32)
    return looked - log_norm


def child_kernel(half_ref, values_ref, table_ref, out_ref, inputs):
    half = half_ref[0]
    values = values_ref[...]
    values = jnp.where(half == 0, values[:, :HALF], values[:, HALF:])
    for k in range(HALF):
        inputs[k] = look_up(values[:, k : k + 1], table_ref[half * HALF + k])
    powers = jnp.zeros((S_LOC, BLK), jnp.float32)
    lanes = lane_of((S_LOC, BLK))
    for k in range(HALF):
        powers = jnp.where(lanes == k, jnp.max(inputs[k], axis=1, keepdims=True), powers)
    powers = jnp.ceil(powers * LOG2E).astype(jnp.bfloat16)
    out_ref[HALF] = powers
    powers = powers.astype(jnp.float32) * LN2
    for k in range(HALF):
        out_ref[k] = jnp.exp(inputs[k] - powers[:, k : k + 1]).astype(jnp.bfloat16)


def pack_kernel(core_ref, own_ref, other_ref, out_ref):
    core = core_ref[0]
    out_ref[pl.ds(core * HALF, HALF)] = own_ref[:HALF]
    out_ref[pl.ds((1 - core) * HALF, HALF)] = other_ref[:HALF]
    own = own_ref[HALF].astype(jnp.float32)
    other = other_ref[HALF].astype(jnp.float32)
    low = jnp.where(core == 0, own, other)
    high = jnp.where(core == 0, other, own)
    powers = jnp.where(lane_of((S_LOC, BLK)) < HALF, low, pltpu.roll(high, HALF, 1))
    out_ref[2 * HALF] = powers.astype(jnp.bfloat16)


def parent_kernel(values_ref, table_ref, prior_ref, out_ref):
    values = values_ref[...]
    for p in range(P_SIZE):
        out_ref[p] = look_up(values[:, p : p + 1], table_ref[p]) + prior_ref[p : p + 1, :]


PLACES = (
    ((0, 0), (3, 0)),
    ((1, 0), (2, 0)),
    ((0, 3), (3, 3)),
    ((1, 3), (2, 3)),
    ((0, 1), (3, 1)),
    ((1, 1), (2, 1)),
    ((0, 2), (3, 2)),
    ((1, 2), (2, 2)),
)


def pick_kernel(code_ref, *refs):
    sources = refs[: len(PLACES)]
    out_refs, pool, powers = refs[len(PLACES) : -2], refs[-2], refs[-1]

    def collect(k, carry):
        for source, places in zip(sources, PLACES):
            for n, (a, b) in enumerate(places):
                pool[(a * 4 + b) * PIECE + k] = source[n * PIECE + k]
        return carry

    lax.fori_loop(0, PIECE, collect, 0)
    for piece in range(16):
        both = pool[piece * PIECE + 2 * HALF].astype(jnp.float32)
        powers[2 * piece] = both
        powers[2 * piece + 1] = pltpu.roll(both, BLK - HALF, 1)
    lanes = lane_of((S_LOC, BLK))
    tops = [jnp.zeros((S_LOC, BLK), jnp.float32)] * 2
    for k in range(HALF):
        for row, out_ref in enumerate(out_refs):
            codes = [code_ref[row * C * NZ // 2 + k * NZ + z] for z in range(NZ)]
            power = [powers[code][:, k : k + 1] for code in codes]
            top = jnp.maximum(jnp.maximum(power[0], power[1]), jnp.maximum(power[2], power[3]))
            tops[row] = jnp.where(lanes == k, top, tops[row])
            for z in range(NZ):
                code = codes[z]
                factor = jnp.broadcast_to(jnp.exp2(power[z] - top), (S_LOC, BLK))
                block = pool[(code // 2) * PIECE + (code % 2) * HALF + k]
                out_ref[k * NZ + z] = (block.astype(jnp.float32) * factor).astype(jnp.bfloat16)
    for row, out_ref in enumerate(out_refs):
        out_ref[HALF * NZ] = tops[row].astype(jnp.bfloat16)


def child_at(core, half, k):
    return jnp.where(core == half, k, HALF + k)


def sums_kernel(
    core_ref, map_ref, own_ref, other_ref, weights_ref, parent_ref, prior_ref,
    stats_ref, root_ref, sums_ref,
):
    core = core_ref[0]
    root_ref[...] = parent_ref[...]
    for half, picked_ref in enumerate((own_ref, other_ref)):
        tops = picked_ref[HALF * NZ].astype(jnp.float32) * LN2
        for k in range(HALF):
            child = child_at(core, half, k)
            row_sums = None
            for z in range(0, NZ, 2):
                picked = jnp.concatenate([picked_ref[k * NZ + z], picked_ref[k * NZ + z + 1]], axis=1)
                wide = jnp.concatenate([weights_ref[child, z], weights_ref[child, z + 1]], axis=1)
                term = lax.dot_general(
                    picked, wide, (((1,), (1,)), ((), ())), preferred_element_type=jnp.float32
                )
                row_sums = term if row_sums is None else row_sums + term
            sums_ref[half * HALF + k] = row_sums
    for half, picked_ref in enumerate((own_ref, other_ref)):
        tops = picked_ref[HALF * NZ].astype(jnp.float32) * LN2
        for k in range(HALF):
            owner = map_ref[child_at(core, half, k)]
            message = jnp.log(sums_ref[half * HALF + k]) + tops[:, k : k + 1]
            root_ref[owner] = root_ref[owner] + message
    lanes = lane_of((S_LOC, BLK))
    prior = prior_ref[...]
    prior_peak = jnp.max(prior, axis=1, keepdims=True)
    prior_total = jnp.sum(jnp.exp(prior - prior_peak), axis=1, keepdims=True)
    eye = lax.broadcasted_iota(jnp.int32, (P_SIZE, BLK), 0)
    wide = lane_of((P_SIZE, BLK))
    stats = jnp.sum(
        jnp.where(wide == eye + 2 * P_SIZE, prior_peak, 0.0)
        + jnp.where(wide == eye + 3 * P_SIZE, prior_total, 0.0),
        axis=0, keepdims=True,
    )
    stats = jnp.broadcast_to(stats, (S_LOC, BLK))
    for p in range(P_SIZE):
        stats = jnp.where(lanes == p, jnp.max(root_ref[p], axis=1, keepdims=True), stats)
    peaks = stats
    for p in range(P_SIZE):
        total = jnp.sum(jnp.exp(root_ref[p] - peaks[:, p : p + 1]), axis=1, keepdims=True)
        stats = jnp.where(lanes == P_SIZE + p, total, stats)
    stats_ref[...] = stats


def merge(stats):
    is_peak = lane_of((S_LOC, BLK)) % (2 * P_SIZE) < P_SIZE
    peaks = [jnp.where(is_peak, s, pltpu.roll(s, P_SIZE, 1)) for s in stats]
    best = peaks[0]
    for p in peaks[1:]:
        best = jnp.maximum(best, p)
    total = None
    for s, p in zip(stats, peaks):
        term = s * jnp.exp(p - best)
        total = term if total is None else total + term
    return jnp.where(is_peak, best, total)


def merge_kernel(*refs):
    refs[-1][...] = merge([r[...] for r in refs[:-1]])


def counts_kernel(scale, n_stats, place_ref, map_ref, *refs):
    stats_refs, refs = refs[:n_stats], refs[n_stats:]
    root_ref, sums_ref, own_ref, other_ref, weights_ref = refs[:5]
    near, far, loglik_ref, posterior = refs[5:12], refs[12:14], refs[14], refs[15]
    core, place = place_ref[0], place_ref[1]
    stats = merge([r[...] for r in stats_refs])
    lanes = lane_of((S_LOC, BLK))
    norm = stats + pltpu.roll(jnp.log(stats), BLK - P_SIZE, 1)
    signed = jnp.where(lanes < P_SIZE, norm, 0.0) - jnp.where(
        (lanes >= 2 * P_SIZE) & (lanes < 3 * P_SIZE), norm, 0.0
    )
    loglik = jnp.sum(signed, axis=1, keepdims=True) / (C + P_SIZE)
    loglik_ref[...] = jnp.broadcast_to(loglik, (S_LOC, BLK))
    for p in range(P_SIZE):
        posterior[p] = jnp.exp(root_ref[p] - norm[:, p : p + 1]).astype(jnp.bfloat16)
    rows = near[0].shape[2]
    parts = BLK // rows
    starts = [pl.multiple_of(lax.rem(place + k, parts) * rows, rows) for k in range(parts)]
    turn = lax.rem(parts - place, parts) * rows
    for half, picked_ref in enumerate((own_ref, other_ref)):
        for k in range(HALF):
            child = child_at(core, half, k)
            share = posterior[map_ref[child]].astype(jnp.float32) / sums_ref[half * HALF + k]
            share = pltpu.roll(share, turn, 1).astype(jnp.bfloat16)
            picked = jnp.concatenate([picked_ref[k * NZ + z] for z in range(NZ)], axis=1)
            flow = lax.dot_general(
                share, picked, (((0,), (0,)), ((), ())), preferred_element_type=jnp.float32
            )
            for distance in range(parts):
                for z in range(NZ):
                    weight = weights_ref[child, z, pl.ds(starts[distance], rows), :]
                    block = flow[distance * rows : (distance + 1) * rows, z * BLK : (z + 1) * BLK]
                    block = (block * (weight.astype(jnp.float32) * scale)).astype(jnp.bfloat16)
                    if distance == 4:
                        far[half][k, z] = block
                    else:
                        near[distance if distance < 4 else distance - 1][half * HALF + k, z] = block


def first_step_kernel(up_ref, down_ref, up_in_ref, down_in_ref, up_out_ref, down_out_ref):
    f32 = jnp.float32
    low, high = pl.ds(0, HALF), pl.ds(HALF, HALF)
    up_out_ref[low] = (up_ref[low].astype(f32) + up_in_ref[...].astype(f32)).astype(jnp.bfloat16)
    up_out_ref[high] = up_ref[high]
    down_out_ref[low] = down_ref[low]
    down_out_ref[high] = (down_ref[high].astype(f32) + down_in_ref[...].astype(f32)).astype(
        jnp.bfloat16
    )


def step_kernel(up_ref, down_ref, up_in_ref, down_in_ref, up_out_ref, down_out_ref):
    f32 = jnp.float32
    up_out_ref[...] = (up_ref[...].astype(f32) + up_in_ref[...].astype(f32)).astype(jnp.bfloat16)
    down_out_ref[...] = (down_ref[...].astype(f32) + down_in_ref[...].astype(f32)).astype(
        jnp.bfloat16
    )


def last_kernel(core_ref, own_ref, up_in_ref, down_in_ref, out_ref):
    f32 = jnp.float32
    core = core_ref[0]
    for half in range(2):
        part = pl.ds(half * HALF, HALF)
        total = own_ref[part].astype(f32) + up_in_ref[part].astype(f32) + down_in_ref[part].astype(f32)
        out_ref[pl.ds(jnp.where(core == half, 0, HALF), HALF)] = total.astype(jnp.bfloat16)


def params(mib):
    return pltpu.CompilerParams(vmem_limit_bytes=mib << 20)


def cost(flops, moved, transcendentals):
    return pl.CostEstimate(flops=flops, bytes_accessed=moved, transcendentals=transcendentals)


def along(a, b):
    pairs = []
    for i in range(32):
        x, y, core = i // 8, i // 2 % 4, i % 2
        dx, dy = (a, b) if core == 0 else (b, a)
        pairs.append((i, (x + dx) % 4 * 8 + (y + dy) % 4 * 2 + core))
    return pairs


SWAP = [(i, i ^ 1) for i in range(32)]


def body(
    child_values,
    parent_values,
    child_logits,
    parent_logits,
    prior_logits,
    weights,
    block_cols,
    parent_map,
):
    f32, bf16, i32 = jnp.float32, jnp.bfloat16, jnp.int32
    shape = jax.ShapeDtypeStruct
    parts = lax.axis_size("batch")
    rows = BLK // parts
    weights = weights[:, 0]
    region = lax.axis_index("region").astype(i32)
    core = lax.rem(region, 2)
    place = jnp.stack([core, lax.axis_index("batch").astype(i32)])

    def scores(half):
        return pl.pallas_call(
            child_kernel,
            out_shape=shape((HALF + 1, S_LOC, BLK), bf16),
            in_specs=[SMEM, VMEM, VMEM],
            out_specs=VMEM,
            scratch_shapes=[pltpu.VMEM((HALF, S_LOC, BLK), f32)],
            compiler_params=params(16),
            cost_estimate=cost(1 << 27, 2 << 20, 1 << 20),
            name="child_scores",
        )(half.reshape(1), child_values, child_logits)

    given = lax.ppermute(scores(1 - core), "region", SWAP)
    kept = scores(core)
    own = pl.pallas_call(
        pack_kernel,
        out_shape=shape((PIECE, S_LOC, BLK), bf16),
        in_specs=[SMEM, VMEM, VMEM],
        out_specs=VMEM,
        compiler_params=params(8),
        name="pack",
    )(place, kept, given)

    def send(value, a, b):
        return lax.ppermute(value, "region", along(a, b))

    parent_in = pl.pallas_call(
        parent_kernel,
        out_shape=shape((P_SIZE, S_LOC, BLK), f32),
        in_specs=[VMEM, VMEM, VMEM],
        out_specs=VMEM,
        compiler_params=params(12),
        cost_estimate=cost(1 << 28, 3 << 20, 1 << 21),
        name="parent_scores",
    )(parent_values, parent_logits, prior_logits)
    columns = block_cols[:, 0]
    columns = jnp.stack([columns, lax.ppermute(columns, "region", SWAP)])
    columns = lax.dynamic_slice_in_dim(columns, core * HALF, HALF, axis=1).reshape(-1)
    x, y = columns // 8 - region // 8 + 4, columns // 2 % 4 - region // 2 % 4 + 4
    x, y = x % 4, y % 4
    code = jnp.where(core == 0, x * 4 + y, y * 4 + x) * 2 + columns % 2

    a1, a3, a2 = send(own, 1, 0), send(own, -1, 0), send(own, 2, 0)
    near = jnp.concatenate([own, a1])
    near_up, near_down = send(near, 0, 1), send(near, 0, -1)
    a3, a2, parent_in, code = lax.optimization_barrier((a3, a2, parent_in, code))
    far = jnp.concatenate([a3, a2])
    far_up, far_down = send(far, 0, 1), send(far, 0, -1)
    next_up = send(near_up, 0, 1)
    next_down = send(far_down, 0, -1)
    picked, for_other = pl.pallas_call(
        pick_kernel,
        out_shape=(shape((HALF * NZ + 1, S_LOC, BLK), bf16),) * 2,
        in_specs=[SMEM] + [VMEM] * len(PLACES),
        out_specs=(VMEM, VMEM),
        scratch_shapes=[
            pltpu.VMEM((16 * PIECE, S_LOC, BLK), bf16),
            pltpu.VMEM((32, S_LOC, BLK), f32),
        ],
        compiler_params=params(22),
        cost_estimate=cost(1 << 22, 20 << 20, 1 << 20),
        name="pick",
    )(code, near, far, near_up, far_up, near_down, far_down, next_up, next_down)
    other = lax.ppermute(for_other, "region", SWAP)
    stats, root, sums = pl.pallas_call(
        sums_kernel,
        out_shape=(
            shape((S_LOC, BLK), f32),
            shape((P_SIZE, S_LOC, BLK), f32),
            shape((C, S_LOC, BLK), f32),
        ),
        in_specs=[SMEM, SMEM] + [VMEM] * 5,
        out_specs=(VMEM,) * 3,
        compiler_params=params(16),
        cost_estimate=cost(1 << 29, 12 << 20, 1 << 20),
        name="row_sums",
    )(place, parent_map, picked, other, weights, parent_in, prior_logits)

    for axis, pairs in (
        ("core", (SWAP,)),
        ("a", tuple(along(step, 0) for step in (1, 3, 2))),
        ("b", tuple(along(0, step) for step in (1, 3, 2))),
    ):
        others = [lax.ppermute(stats, "region", p) for p in pairs]
        if axis == "b":
            break
        stats = pl.pallas_call(
            merge_kernel,
            out_shape=shape((S_LOC, BLK), f32),
            in_specs=[VMEM] * (1 + len(others)),
            out_specs=VMEM,
            compiler_params=params(4),
            name="merge_" + axis,
        )(stats, *others)
    scale = K * NZ * BLK / (S_LOC * parts)
    whole, half_set = shape((C, NZ, rows, BLK), bf16), shape((HALF, NZ, rows, BLK), bf16)
    n0, n1, n2, n3, n5, n6, n7, far_up, far_down, loglik = pl.pallas_call(
        lambda *refs: counts_kernel(scale, 1 + len(others), *refs),
        out_shape=(whole,) * 7 + (half_set,) * 2 + (shape((S_LOC, BLK), f32),),
        in_specs=[SMEM, SMEM] + [VMEM] * (6 + len(others)),
        out_specs=(VMEM,) * 10,
        scratch_shapes=[pltpu.VMEM((P_SIZE, S_LOC, BLK), bf16)],
        compiler_params=params(24),
        cost_estimate=cost(1 << 29, 13 << 20, 1 << 19),
        name="counts",
    )(place, parent_map, stats, *others, root, sums, picked, other, weights)

    def ring(up, down):
        shift = lambda step: [(i, (i + step) % parts) for i in range(parts)]
        return lax.ppermute(up, "batch", shift(1)), lax.ppermute(down, "batch", shift(-1))

    up, down = ring(far_up, far_down)
    for kernel, here_up, here_down in (
        (first_step_kernel, n3, n5),
        (step_kernel, n2, n6),
        (step_kernel, n1, n7),
    ):
        up, down = ring(
            *pl.pallas_call(
                kernel,
                out_shape=(whole, whole),
                in_specs=[VMEM] * 4,
                out_specs=(VMEM, VMEM),
                compiler_params=params(8),
                name="ring_add",
            )(here_up, here_down, up, down)
        )
    counts = pl.pallas_call(
        last_kernel,
        out_shape=whole,
        in_specs=[SMEM] + [VMEM] * 3,
        out_specs=VMEM,
        compiler_params=params(8),
        name="ring_last",
    )(place, n0, up, down)
    return (counts[:, None], loglik[:, 0])


def solution(mesh):
    return jax.shard_map(
        body,
        mesh=mesh,
        in_specs=(
            P("batch", None),
            P("batch", None),
            P(None, None, "region"),
            P(None, None, "region"),
            P(None, "region"),
            P(None, "region", None, None, None),
            P(None, "region", None),
            P(),
        ),
        out_specs=(P(None, "region", None, "batch", None), P("batch")),
        check_vma=False,
    )
```

```python
import jax
import jax.numpy as jnp
from jax import lax
from jax.experimental import pallas as pl
from jax.experimental.pallas import tpu as pltpu
from jax.sharding import PartitionSpec as P

K = 4096
BLK = 128
NZ = 4
C = 32
P_SIZE = 32
S_LOC = 64
LN2 = 0.6931471805599453
LOG2E = 1.4426950408889634
HALF = C // 2
PIECE = 2 * HALF + 1
VMEM = pl.BlockSpec(memory_space=pltpu.VMEM)
SMEM = pl.BlockSpec(memory_space=pltpu.SMEM)
ANY = pl.BlockSpec(memory_space=pl.ANY)


def lane_of(shape):
    return lax.broadcasted_iota(jnp.int32, shape, len(shape) - 1)


def look_up(values, table):
    wide = table.astype(jnp.float32)
    top = jnp.max(wide, axis=0, keepdims=True)
    log_norm = jnp.log(jnp.sum(jnp.exp(wide - top), axis=0, keepdims=True)) + top
    hot = (values == lane_of((S_LOC, table.shape[0]))).astype(jnp.float32)
    looked = jnp.dot(hot.astype(jnp.bfloat16), table, preferred_element_type=jnp.float32)
    return looked - log_norm


def child_kernel(half_ref, values_ref, table_ref, out_ref, inputs):
    half = half_ref[0]
    values = values_ref[...].T
    values = jnp.where(half == 0, values[:, :HALF], values[:, HALF:])
    for k in range(HALF):
        inputs[k] = look_up(values[:, k : k + 1], table_ref[half * HALF + k])
    powers = jnp.zeros((S_LOC, BLK), jnp.float32)
    lanes = lane_of((S_LOC, BLK))
    for k in range(HALF):
        powers = jnp.where(lanes == k, jnp.max(inputs[k], axis=1, keepdims=True), powers)
    powers = jnp.ceil(powers * LOG2E).astype(jnp.bfloat16)
    out_ref[HALF] = powers
    powers = powers.astype(jnp.float32) * LN2
    for k in range(HALF):
        out_ref[k] = jnp.exp(inputs[k] - powers[:, k : k + 1]).astype(jnp.bfloat16)


def pack_kernel(core_ref, own_ref, other_ref, out_ref):
    core = core_ref[0]
    out_ref[pl.ds(core * HALF, HALF)] = own_ref[:HALF]
    out_ref[pl.ds((1 - core) * HALF, HALF)] = other_ref[:HALF]
    own = own_ref[HALF].astype(jnp.float32)
    other = other_ref[HALF].astype(jnp.float32)
    low = jnp.where(core == 0, own, other)
    high = jnp.where(core == 0, other, own)
    powers = jnp.where(lane_of((S_LOC, BLK)) < HALF, low, pltpu.roll(high, HALF, 1))
    out_ref[2 * HALF] = powers.astype(jnp.bfloat16)


def parent_kernel(values_ref, table_ref, prior_ref, out_ref):
    values = values_ref[...].T
    for p in range(P_SIZE):
        out_ref[p] = look_up(values[:, p : p + 1], table_ref[p]) + prior_ref[p : p + 1, :]


PLACES = (
    ((0, 0), (3, 0)),
    ((1, 0), (2, 0)),
    ((0, 3), (3, 3)),
    ((1, 3), (2, 3)),
    ((0, 1), (3, 1)),
    ((1, 1), (2, 1)),
    ((0, 2), (3, 2)),
    ((1, 2), (2, 2)),
)


def codes_of(place_ref, columns_ref, k):
    core = place_ref[0]
    codes = []
    for z in range(NZ):
        column = columns_ref[z, core * HALF + k]
        x, y = lax.shift_right_logical(column, 3), lax.shift_right_logical(column, 1) & 3
        a = (jnp.where(core == 0, x, y) - place_ref[2]) & 3
        b = (jnp.where(core == 0, y, x) - place_ref[3]) & 3
        codes.append((a * 4 + b) * 2 + (column & 1))
    return codes


def pick_child(codes, k, pool, powers):
    power = [powers[code][:, k : k + 1] for code in codes]
    top = jnp.maximum(jnp.maximum(power[0], power[1]), jnp.maximum(power[2], power[3]))
    blocks = []
    for code, mine in zip(codes, power):
        factor = jnp.broadcast_to(jnp.exp2(mine - top), (S_LOC, BLK))
        block = pool[lax.shift_right_logical(code, 1) * PIECE + (code & 1) * HALF + k]
        blocks.append((block.astype(jnp.float32) * factor).astype(jnp.bfloat16))
    return blocks, top


def pick_other_kernel(place_ref, columns_ref, *refs):
    sources, (out_ref, pool, powers) = refs[: len(PLACES)], refs[len(PLACES) :]

    def collect(k, carry):
        for source, places in zip(sources, PLACES):
            for n, (a, b) in enumerate(places):
                pool[(a * 4 + b) * PIECE + k] = source[n * PIECE + k]
        return carry

    lax.fori_loop(0, PIECE, collect, 0)
    for piece in range(16):
        both = pool[piece * PIECE + 2 * HALF].astype(jnp.float32)
        powers[2 * piece] = both
        powers[2 * piece + 1] = pltpu.roll(both, BLK - HALF, 1)
    lanes = lane_of((S_LOC, BLK))
    tops = jnp.zeros((S_LOC, BLK), jnp.float32)
    for k in range(HALF):
        blocks, top = pick_child(codes_of(place_ref, columns_ref, k), k, pool, powers)
        tops = jnp.where(lanes == k, top, tops)
        for z in range(NZ):
            out_ref[k * NZ + z] = blocks[z]
    out_ref[HALF * NZ] = tops.astype(jnp.bfloat16)


def row_sum(blocks, weights_ref, child):
    total = None
    for z in range(0, NZ, 2):
        picked = jnp.concatenate(blocks[z : z + 2], axis=1)
        wide = jnp.concatenate([weights_ref[child, z], weights_ref[child, z + 1]], axis=1)
        term = lax.dot_general(
            picked, wide, (((1,), (1,)), ((), ())), preferred_element_type=jnp.float32
        )
        total = term if total is None else total + term
    return total


def own_sums_kernel(place_ref, columns_ref, pool, powers, weights_ref, out_ref, sums_ref):
    lanes = lane_of((S_LOC, BLK))
    tops = jnp.zeros((S_LOC, BLK), jnp.float32)
    for k in range(HALF):
        blocks, top = pick_child(codes_of(place_ref, columns_ref, k), k, pool, powers)
        tops = jnp.where(lanes == k, top, tops)
        for z in range(NZ):
            out_ref[k * NZ + z] = blocks[z]
        sums_ref[k] = row_sum(blocks, weights_ref, child_at(place_ref[0], 0, k))
    out_ref[HALF * NZ] = tops.astype(jnp.bfloat16)


def child_at(core, half, k):
    return jnp.where(core == half, k, HALF + k)


def sums_kernel(
    core_ref, map_ref, own_ref, other_ref, own_sums_ref, weights_ref, parent_ref, prior_ref,
    stats_ref, root_ref, sums_ref,
):
    core = core_ref[0]
    root_ref[...] = parent_ref[...]
    for k in range(HALF):
        sums_ref[k] = own_sums_ref[k]
        blocks = [other_ref[k * NZ + z] for z in range(NZ)]
        sums_ref[HALF + k] = row_sum(blocks, weights_ref, child_at(core, 1, k))
    for half, picked_ref in enumerate((own_ref, other_ref)):
        tops = picked_ref[HALF * NZ].astype(jnp.float32) * LN2
        for k in range(HALF):
            owner = map_ref[child_at(core, half, k)]
            message = jnp.log(sums_ref[half * HALF + k]) + tops[:, k : k + 1]
            root_ref[owner] = root_ref[owner] + message
    lanes = lane_of((S_LOC, BLK))
    prior = prior_ref[...]
    prior_peak = jnp.max(prior, axis=1, keepdims=True)
    prior_total = jnp.sum(jnp.exp(prior - prior_peak), axis=1, keepdims=True)
    eye = lax.broadcasted_iota(jnp.int32, (P_SIZE, BLK), 0)
    wide = lane_of((P_SIZE, BLK))
    stats = jnp.sum(
        jnp.where(wide == eye + 2 * P_SIZE, prior_peak, 0.0)
        + jnp.where(wide == eye + 3 * P_SIZE, prior_total, 0.0),
        axis=0, keepdims=True,
    )
    stats = jnp.broadcast_to(stats, (S_LOC, BLK))
    for p in range(P_SIZE):
        stats = jnp.where(lanes == p, jnp.max(root_ref[p], axis=1, keepdims=True), stats)
    peaks = stats
    for p in range(P_SIZE):
        total = jnp.sum(jnp.exp(root_ref[p] - peaks[:, p : p + 1]), axis=1, keepdims=True)
        stats = jnp.where(lanes == P_SIZE + p, total, stats)
    stats_ref[...] = stats


def merge(stats):
    is_peak = lane_of((S_LOC, BLK)) % (2 * P_SIZE) < P_SIZE
    peaks = [jnp.where(is_peak, s, pltpu.roll(s, P_SIZE, 1)) for s in stats]
    best = peaks[0]
    for p in peaks[1:]:
        best = jnp.maximum(best, p)
    total = None
    for s, p in zip(stats, peaks):
        term = s * jnp.exp(p - best)
        total = term if total is None else total + term
    return jnp.where(is_peak, best, total)


def merge_kernel(*refs):
    refs[-1][...] = merge([r[...] for r in refs[:-1]])


def counts_kernel(scale, n_stats, place_ref, map_ref, *refs):
    stats_refs, refs = refs[:n_stats], refs[n_stats:]
    root_ref, sums_ref, own_ref, other_ref, weights_ref = refs[:5]
    near, far, loglik_ref, posterior = refs[5:12], refs[12:14], refs[14], refs[15]
    core, place = place_ref[0], place_ref[1]
    stats = merge([r[...] for r in stats_refs])
    lanes = lane_of((S_LOC, BLK))
    norm = stats + pltpu.roll(jnp.log(stats), BLK - P_SIZE, 1)
    signed = jnp.where(lanes < P_SIZE, norm, 0.0) - jnp.where(
        (lanes >= 2 * P_SIZE) & (lanes < 3 * P_SIZE), norm, 0.0
    )
    loglik = jnp.sum(signed, axis=1, keepdims=True) / (C + P_SIZE)
    loglik_ref[...] = jnp.broadcast_to(loglik, (S_LOC, BLK))
    for p in range(P_SIZE):
        posterior[p] = jnp.exp(root_ref[p] - norm[:, p : p + 1]).astype(jnp.bfloat16)
    rows = near[0].shape[2]
    parts = BLK // rows
    starts = [pl.multiple_of(lax.rem(place + k, parts) * rows, rows) for k in range(parts)]
    turn = lax.rem(parts - place, parts) * rows
    for half, picked_ref in enumerate((own_ref, other_ref)):
        for k in range(HALF):
            child = child_at(core, half, k)
            share = posterior[map_ref[child]].astype(jnp.float32) / sums_ref[half * HALF + k]
            share = pltpu.roll(share, turn, 1).astype(jnp.bfloat16)
            picked = jnp.concatenate([picked_ref[k * NZ + z] for z in range(NZ)], axis=1)
            flow = lax.dot_general(
                share, picked, (((0,), (0,)), ((), ())), preferred_element_type=jnp.float32
            )
            for distance in range(parts):
                for z in range(NZ):
                    weight = weights_ref[child, z, pl.ds(starts[distance], rows), :]
                    block = flow[distance * rows : (distance + 1) * rows, z * BLK : (z + 1) * BLK]
                    block = (block * (weight.astype(jnp.float32) * scale)).astype(jnp.bfloat16)
                    if distance == 4:
                        far[half][k, z] = block
                    else:
                        near[distance if distance < 4 else distance - 1][half * HALF + k, z] = block


def first_step_kernel(up_ref, down_ref, up_in_ref, down_in_ref, up_out_ref, down_out_ref):
    f32 = jnp.float32
    low, high = pl.ds(0, HALF), pl.ds(HALF, HALF)
    up_out_ref[low] = (up_ref[low].astype(f32) + up_in_ref[...].astype(f32)).astype(jnp.bfloat16)
    up_out_ref[high] = up_ref[high]
    down_out_ref[low] = down_ref[low]
    down_out_ref[high] = (down_ref[high].astype(f32) + down_in_ref[...].astype(f32)).astype(
        jnp.bfloat16
    )


def step_kernel(up_ref, down_ref, up_in_ref, down_in_ref, up_out_ref, down_out_ref):
    f32 = jnp.float32
    up_out_ref[...] = (up_ref[...].astype(f32) + up_in_ref[...].astype(f32)).astype(jnp.bfloat16)
    down_out_ref[...] = (down_ref[...].astype(f32) + down_in_ref[...].astype(f32)).astype(
        jnp.bfloat16
    )


def last_kernel(core_ref, own_ref, up_in_ref, down_in_ref, out_ref):
    f32 = jnp.float32
    core = core_ref[0]
    for half in range(2):
        part = pl.ds(half * HALF, HALF)
        total = own_ref[part].astype(f32) + up_in_ref[part].astype(f32) + down_in_ref[part].astype(f32)
        out_ref[pl.ds(jnp.where(core == half, 0, HALF), HALF)] = total.astype(jnp.bfloat16)


def params(mib):
    return pltpu.CompilerParams(vmem_limit_bytes=mib << 20)


def cost(flops, moved, transcendentals):
    return pl.CostEstimate(flops=flops, bytes_accessed=moved, transcendentals=transcendentals)


def along(a, b):
    pairs = []
    for i in range(32):
        x, y, core = i // 8, i // 2 % 4, i % 2
        dx, dy = (a, b) if core == 0 else (b, a)
        pairs.append((i, (x + dx) % 4 * 8 + (y + dy) % 4 * 2 + core))
    return pairs


SWAP = [(i, i ^ 1) for i in range(32)]


def body(
    child_values,
    parent_values,
    child_logits,
    parent_logits,
    prior_logits,
    weights,
    block_cols,
    parent_map,
):
    f32, bf16, i32 = jnp.float32, jnp.bfloat16, jnp.int32
    shape = jax.ShapeDtypeStruct
    parts = lax.axis_size("batch")
    rows = BLK // parts
    weights = weights[:, 0]
    region = lax.axis_index("region").astype(i32)
    core = lax.rem(region, 2)
    x, y = lax.shift_right_logical(region, 3), lax.shift_right_logical(region, 1) & 3
    place = jnp.stack(
        [
            core,
            lax.axis_index("batch").astype(i32),
            jnp.where(core == 0, x, y),
            jnp.where(core == 0, y, x),
        ]
    )

    columns = block_cols[:, 0].T

    def scores(half):
        return pl.pallas_call(
            child_kernel,
            out_shape=shape((HALF + 1, S_LOC, BLK), bf16),
            in_specs=[SMEM, VMEM, VMEM],
            out_specs=VMEM,
            scratch_shapes=[pltpu.VMEM((HALF, S_LOC, BLK), f32)],
            compiler_params=params(16),
            cost_estimate=cost(1 << 27, 2 << 20, 1 << 20),
            name="child_scores",
        )(half.reshape(1), child_values.T, child_logits)

    given, other_columns = lax.optimization_barrier(
        (lax.ppermute(scores(1 - core), "region", SWAP), lax.ppermute(columns, "region", SWAP))
    )
    kept = scores(core)
    own = pl.pallas_call(
        pack_kernel,
        out_shape=shape((PIECE, S_LOC, BLK), bf16),
        in_specs=[SMEM, VMEM, VMEM],
        out_specs=VMEM,
        compiler_params=params(8),
        name="pack",
    )(place, kept, given)

    def send(value, a, b):
        return lax.ppermute(value, "region", along(a, b))

    parent_in = pl.pallas_call(
        parent_kernel,
        out_shape=shape((P_SIZE, S_LOC, BLK), f32),
        in_specs=[VMEM, VMEM, VMEM],
        out_specs=VMEM,
        compiler_params=params(12),
        cost_estimate=cost(1 << 28, 3 << 20, 1 << 21),
        name="parent_scores",
    )(parent_values.T, parent_logits, prior_logits)
    a1, a3 = send(own, 1, 0), send(own, -1, 0)
    a1, own = lax.optimization_barrier((a1, own))
    a2 = send(own, 2, 0)
    near = jnp.concatenate([own, a1])
    near_up, near_down = send(near, 0, 1), send(near, 0, -1)
    far = jnp.concatenate([a3, a2])
    far_up, far_down = send(far, 0, 1), send(far, 0, -1)
    next_up = send(near_up, 0, 1)
    next_down = send(far_down, 0, -1)
    slots = shape((HALF * NZ + 1, S_LOC, BLK), bf16)
    for_other, pool, powers = pl.pallas_call(
        pick_other_kernel,
        out_shape=(
            slots,
            shape((16 * PIECE, S_LOC, BLK), bf16),
            shape((32, S_LOC, BLK), f32),
        ),
        in_specs=[SMEM, SMEM] + [VMEM] * len(PLACES),
        out_specs=(VMEM, VMEM, VMEM),
        compiler_params=params(22),
        cost_estimate=cost(1 << 22, 20 << 20, 1 << 20),
        name="pick_other",
    )(place, other_columns, near, far, near_up, far_up, near_down, far_down, next_up, next_down)
    other = lax.ppermute(for_other, "region", SWAP)
    picked, own_sums = pl.pallas_call(
        own_sums_kernel,
        out_shape=(slots, shape((HALF, S_LOC, BLK), f32)),
        in_specs=[SMEM, SMEM] + [VMEM] * 3,
        out_specs=(VMEM, VMEM),
        compiler_params=params(20),
        cost_estimate=cost(1 << 28, 8 << 20, 1 << 19),
        name="own_sums",
    )(place, columns, pool, powers, weights)
    stats, root, sums = pl.pallas_call(
        sums_kernel,
        out_shape=(
            shape((S_LOC, BLK), f32),
            shape((P_SIZE, S_LOC, BLK), f32),
            shape((C, S_LOC, BLK), f32),
        ),
        in_specs=[SMEM, SMEM] + [VMEM] * 6,
        out_specs=(VMEM,) * 3,
        compiler_params=params(16),
        cost_estimate=cost(1 << 29, 12 << 20, 1 << 20),
        name="row_sums",
    )(place, parent_map, picked, other, own_sums, weights, parent_in, prior_logits)

    for axis, pairs in (
        ("core", (SWAP,)),
        ("a", tuple(along(step, 0) for step in (1, 3, 2))),
        ("b", tuple(along(0, step) for step in (1, 3, 2))),
    ):
        others = [lax.ppermute(stats, "region", p) for p in pairs]
        if axis == "b":
            break
        stats = pl.pallas_call(
            merge_kernel,
            out_shape=shape((S_LOC, BLK), f32),
            in_specs=[VMEM] * (1 + len(others)),
            out_specs=VMEM,
            compiler_params=params(4),
            name="merge_" + axis,
        )(stats, *others)
    scale = K * NZ * BLK / (S_LOC * parts)
    whole, half_set = shape((C, NZ, rows, BLK), bf16), shape((HALF, NZ, rows, BLK), bf16)
    n0, n1, n2, n3, n5, n6, n7, far_up, far_down, loglik = pl.pallas_call(
        lambda *refs: counts_kernel(scale, 1 + len(others), *refs),
        out_shape=(whole,) * 7 + (half_set,) * 2 + (shape((S_LOC, BLK), f32),),
        in_specs=[SMEM, SMEM] + [VMEM] * (6 + len(others)),
        out_specs=(VMEM,) * 10,
        scratch_shapes=[pltpu.VMEM((P_SIZE, S_LOC, BLK), bf16)],
        compiler_params=params(24),
        cost_estimate=cost(1 << 29, 13 << 20, 1 << 19),
        name="counts",
    )(place, parent_map, stats, *others, root, sums, picked, other, weights)

    def ring(up, down):
        shift = lambda step: [(i, (i + step) % parts) for i in range(parts)]
        return lax.ppermute(up, "batch", shift(1)), lax.ppermute(down, "batch", shift(-1))

    up, down = ring(far_up, far_down)
    for kernel, here_up, here_down in (
        (first_step_kernel, n3, n5),
        (step_kernel, n2, n6),
        (step_kernel, n1, n7),
    ):
        up, down = ring(
            *pl.pallas_call(
                kernel,
                out_shape=(whole, whole),
                in_specs=[VMEM] * 4,
                out_specs=(VMEM, VMEM),
                compiler_params=params(8),
                name="ring_add",
            )(here_up, here_down, up, down)
        )
    counts = pl.pallas_call(
        last_kernel,
        out_shape=whole,
        in_specs=[SMEM] + [VMEM] * 3,
        out_specs=VMEM,
        compiler_params=params(8),
        name="ring_last",
    )(place, n0, up, down)
    return (counts[:, None], loglik[:, 0])


def solution(mesh):
    return jax.shard_map(
        body,
        mesh=mesh,
        in_specs=(
            P("batch", None),
            P("batch", None),
            P(None, None, "region"),
            P(None, None, "region"),
            P(None, "region"),
            P(None, "region", None, None, None),
            P(None, "region", None),
            P(),
        ),
        out_specs=(P(None, "region", None, "batch", None), P("batch")),
        check_vma=False,
    )
```

```python
import jax
import jax.numpy as jnp
from jax import lax
from jax.experimental import pallas as pl
from jax.experimental.pallas import tpu as pltpu
from jax.sharding import PartitionSpec as P

K = 4096
BLK = 128
NZ = 4
C = 32
P_SIZE = 32
S_LOC = 64
LN2 = 0.6931471805599453
LOG2E = 1.4426950408889634
HALF = C // 2
PIECE = 2 * HALF + 1
VMEM = pl.BlockSpec(memory_space=pltpu.VMEM)
SMEM = pl.BlockSpec(memory_space=pltpu.SMEM)
ANY = pl.BlockSpec(memory_space=pl.ANY)


def lane_of(shape):
    return lax.broadcasted_iota(jnp.int32, shape, len(shape) - 1)


def look_up(values, table):
    wide = table.astype(jnp.float32)
    top = jnp.max(wide, axis=0, keepdims=True)
    log_norm = jnp.log(jnp.sum(jnp.exp(wide - top), axis=0, keepdims=True)) + top
    hot = (values == lane_of((S_LOC, table.shape[0]))).astype(jnp.float32)
    looked = jnp.dot(hot.astype(jnp.bfloat16), table, preferred_element_type=jnp.float32)
    return looked - log_norm


def child_kernel(half_ref, values_ref, table_ref, out_ref, inputs):
    half = half_ref[0]
    values = values_ref[...].T
    values = jnp.where(half == 0, values[:, :HALF], values[:, HALF:])
    for k in range(HALF):
        inputs[k] = look_up(values[:, k : k + 1], table_ref[half * HALF + k])
    powers = jnp.zeros((S_LOC, BLK), jnp.float32)
    lanes = lane_of((S_LOC, BLK))
    for k in range(HALF):
        powers = jnp.where(lanes == k, jnp.max(inputs[k], axis=1, keepdims=True), powers)
    powers = jnp.ceil(powers * LOG2E).astype(jnp.bfloat16)
    out_ref[HALF] = powers
    powers = powers.astype(jnp.float32) * LN2
    for k in range(HALF):
        out_ref[k] = jnp.exp(inputs[k] - powers[:, k : k + 1]).astype(jnp.bfloat16)


def pack_kernel(core_ref, own_ref, other_ref, out_ref):
    core = core_ref[0]
    out_ref[pl.ds(core * HALF, HALF)] = own_ref[:HALF]
    out_ref[pl.ds((1 - core) * HALF, HALF)] = other_ref[:HALF]
    own = own_ref[HALF].astype(jnp.float32)
    other = other_ref[HALF].astype(jnp.float32)
    low = jnp.where(core == 0, own, other)
    high = jnp.where(core == 0, other, own)
    powers = jnp.where(lane_of((S_LOC, BLK)) < HALF, low, pltpu.roll(high, HALF, 1))
    out_ref[2 * HALF] = powers.astype(jnp.bfloat16)


def parent_kernel(values_ref, table_ref, prior_ref, out_ref):
    values = values_ref[...].T
    for p in range(P_SIZE):
        out_ref[p] = look_up(values[:, p : p + 1], table_ref[p]) + prior_ref[p : p + 1, :]


PLACES = (
    ((0, 0), (3, 0)),
    ((1, 0), (2, 0)),
    ((0, 3), (3, 3)),
    ((1, 3), (2, 3)),
    ((0, 1), (3, 1)),
    ((1, 1), (2, 1)),
    ((0, 2), (3, 2)),
    ((1, 2), (2, 2)),
)


def codes_of(place_ref, columns_ref, k):
    core = place_ref[0]
    codes = []
    for z in range(NZ):
        column = columns_ref[z, core * HALF + k]
        x, y = lax.shift_right_logical(column, 3), lax.shift_right_logical(column, 1) & 3
        a = (jnp.where(core == 0, x, y) - place_ref[2]) & 3
        b = (jnp.where(core == 0, y, x) - place_ref[3]) & 3
        codes.append((a * 4 + b) * 2 + (column & 1))
    return codes


def pick_child(codes, k, pool, powers):
    power = [powers[code][:, k : k + 1] for code in codes]
    top = jnp.maximum(jnp.maximum(power[0], power[1]), jnp.maximum(power[2], power[3]))
    blocks = []
    for code, mine in zip(codes, power):
        factor = jnp.broadcast_to(jnp.exp2(mine - top), (S_LOC, BLK))
        block = pool[lax.shift_right_logical(code, 1) * PIECE + (code & 1) * HALF + k]
        blocks.append((block.astype(jnp.float32) * factor).astype(jnp.bfloat16))
    return blocks, top


def pick_other_kernel(place_ref, columns_ref, *refs):
    sources, (out_ref, pool, powers) = refs[: len(PLACES)], refs[len(PLACES) :]

    def collect(k, carry):
        for source, places in zip(sources, PLACES):
            for n, (a, b) in enumerate(places):
                pool[(a * 4 + b) * PIECE + k] = source[n * PIECE + k]
        return carry

    lax.fori_loop(0, PIECE, collect, 0)
    for piece in range(16):
        both = pool[piece * PIECE + 2 * HALF].astype(jnp.float32)
        powers[2 * piece] = both
        powers[2 * piece + 1] = pltpu.roll(both, BLK - HALF, 1)
    lanes = lane_of((S_LOC, BLK))
    tops = jnp.zeros((S_LOC, BLK), jnp.float32)
    for k in range(HALF):
        blocks, top = pick_child(codes_of(place_ref, columns_ref, k), k, pool, powers)
        tops = jnp.where(lanes == k, top, tops)
        for z in range(NZ):
            out_ref[k * NZ + z] = blocks[z]
    out_ref[HALF * NZ] = tops.astype(jnp.bfloat16)


def row_sum(blocks, weights_ref, child):
    total = None
    for z in range(0, NZ, 2):
        picked = jnp.concatenate(blocks[z : z + 2], axis=1)
        wide = jnp.concatenate([weights_ref[child, z], weights_ref[child, z + 1]], axis=1)
        term = lax.dot_general(
            picked, wide, (((1,), (1,)), ((), ())), preferred_element_type=jnp.float32
        )
        total = term if total is None else total + term
    return total


def child_at(core, half, k):
    return jnp.where(core == half, k, HALF + k)


def own_sums_kernel(
    place_ref, columns_ref, map_ref, pool, powers, weights_ref, parent_ref,
    out_ref, sums_ref, root_ref,
):
    root_ref[...] = parent_ref[...]
    for k in range(HALF):
        child = child_at(place_ref[0], 0, k)
        blocks, top = pick_child(codes_of(place_ref, columns_ref, k), k, pool, powers)
        for z in range(NZ):
            out_ref[k * NZ + z] = blocks[z]
        row_sums = row_sum(blocks, weights_ref, child)
        sums_ref[k] = row_sums
        owner = map_ref[child]
        root_ref[owner] = root_ref[owner] + (jnp.log(row_sums) + top * LN2)


def sums_kernel(
    place_ref, map_ref, other_ref, weights_ref, own_root_ref, prior_ref,
    stats_ref, root_ref, sums_ref,
):
    root_ref[...] = own_root_ref[...]
    tops = other_ref[HALF * NZ].astype(jnp.float32) * LN2
    for k in range(HALF):
        child = child_at(place_ref[0], 1, k)
        row_sums = row_sum([other_ref[k * NZ + z] for z in range(NZ)], weights_ref, child)
        sums_ref[k] = row_sums
        owner = map_ref[child]
        root_ref[owner] = root_ref[owner] + (jnp.log(row_sums) + tops[:, k : k + 1])
    lanes = lane_of((S_LOC, BLK))
    prior = prior_ref[...]
    prior_peak = jnp.max(prior, axis=1, keepdims=True)
    prior_total = jnp.sum(jnp.exp(prior - prior_peak), axis=1, keepdims=True)
    eye = lax.broadcasted_iota(jnp.int32, (P_SIZE, BLK), 0)
    wide = lane_of((P_SIZE, BLK))
    stats = jnp.sum(
        jnp.where(wide == eye + 2 * P_SIZE, prior_peak, 0.0)
        + jnp.where(wide == eye + 3 * P_SIZE, prior_total, 0.0),
        axis=0, keepdims=True,
    )
    stats = jnp.broadcast_to(stats, (S_LOC, BLK))
    peaks = [jnp.max(root_ref[p], axis=1, keepdims=True) for p in range(P_SIZE)]
    for p in range(P_SIZE):
        total = jnp.sum(jnp.exp(root_ref[p] - peaks[p]), axis=1, keepdims=True)
        stats = jnp.where(lanes == p, peaks[p], stats)
        stats = jnp.where(lanes == P_SIZE + p, total, stats)
    stats_ref[...] = stats


def merge(stats):
    is_peak = lane_of((S_LOC, BLK)) % (2 * P_SIZE) < P_SIZE
    peaks = [jnp.where(is_peak, s, pltpu.roll(s, P_SIZE, 1)) for s in stats]
    best = peaks[0]
    for p in peaks[1:]:
        best = jnp.maximum(best, p)
    total = None
    for s, p in zip(stats, peaks):
        term = s * jnp.exp(p - best)
        total = term if total is None else total + term
    return jnp.where(is_peak, best, total)


def merge_kernel(*refs):
    refs[-1][...] = merge([r[...] for r in refs[:-1]])


def counts_kernel(scale, n_stats, place_ref, map_ref, *refs):
    stats_refs, refs = refs[:n_stats], refs[n_stats:]
    root_ref, own_sums_ref, other_sums_ref, own_ref, other_ref, weights_ref = refs[:6]
    near, far, loglik_ref, posterior = refs[6:13], refs[13:15], refs[15], refs[16]
    core, place = place_ref[0], place_ref[1]
    stats = merge([r[...] for r in stats_refs])
    lanes = lane_of((S_LOC, BLK))
    norm = stats + pltpu.roll(jnp.log(stats), BLK - P_SIZE, 1)
    signed = jnp.where(lanes < P_SIZE, norm, 0.0) - jnp.where(
        (lanes >= 2 * P_SIZE) & (lanes < 3 * P_SIZE), norm, 0.0
    )
    loglik = jnp.sum(signed, axis=1, keepdims=True) / (C + P_SIZE)
    loglik_ref[...] = jnp.broadcast_to(loglik, (S_LOC, BLK))
    for p in range(P_SIZE):
        posterior[p] = jnp.exp(root_ref[p] - norm[:, p : p + 1]).astype(jnp.bfloat16)
    rows = near[0].shape[2]
    parts = BLK // rows
    starts = [pl.multiple_of(lax.rem(place + k, parts) * rows, rows) for k in range(parts)]
    turn = lax.rem(parts - place, parts) * rows
    for half, (picked_ref, sums_ref) in enumerate(
        ((own_ref, own_sums_ref), (other_ref, other_sums_ref))
    ):
        for k in range(HALF):
            child = child_at(core, half, k)
            share = posterior[map_ref[child]].astype(jnp.float32) / sums_ref[k]
            share = pltpu.roll(share, turn, 1).astype(jnp.bfloat16)
            picked = jnp.concatenate([picked_ref[k * NZ + z] for z in range(NZ)], axis=1)
            flow = lax.dot_general(
                share, picked, (((0,), (0,)), ((), ())), preferred_element_type=jnp.float32
            )
            for distance in range(parts):
                for z in range(NZ):
                    weight = weights_ref[child, z, pl.ds(starts[distance], rows), :]
                    block = flow[distance * rows : (distance + 1) * rows, z * BLK : (z + 1) * BLK]
                    block = (block * (weight.astype(jnp.float32) * scale)).astype(jnp.bfloat16)
                    if distance == 4:
                        far[half][k, z] = block
                    else:
                        near[distance if distance < 4 else distance - 1][half * HALF + k, z] = block


def first_step_kernel(up_ref, down_ref, up_in_ref, down_in_ref, up_out_ref, down_out_ref):
    f32 = jnp.float32
    low, high = pl.ds(0, HALF), pl.ds(HALF, HALF)
    up_out_ref[low] = (up_ref[low].astype(f32) + up_in_ref[...].astype(f32)).astype(jnp.bfloat16)
    up_out_ref[high] = up_ref[high]
    down_out_ref[low] = down_ref[low]
    down_out_ref[high] = (down_ref[high].astype(f32) + down_in_ref[...].astype(f32)).astype(
        jnp.bfloat16
    )


def step_kernel(up_ref, down_ref, up_in_ref, down_in_ref, up_out_ref, down_out_ref):
    f32 = jnp.float32
    up_out_ref[...] = (up_ref[...].astype(f32) + up_in_ref[...].astype(f32)).astype(jnp.bfloat16)
    down_out_ref[...] = (down_ref[...].astype(f32) + down_in_ref[...].astype(f32)).astype(
        jnp.bfloat16
    )


def last_kernel(core_ref, own_ref, up_in_ref, down_in_ref, out_ref):
    f32 = jnp.float32
    core = core_ref[0]
    for half in range(2):
        part = pl.ds(half * HALF, HALF)
        total = own_ref[part].astype(f32) + up_in_ref[part].astype(f32) + down_in_ref[part].astype(f32)
        out_ref[pl.ds(jnp.where(core == half, 0, HALF), HALF)] = total.astype(jnp.bfloat16)


def params(mib):
    return pltpu.CompilerParams(vmem_limit_bytes=mib << 20)


def cost(flops, moved, transcendentals):
    return pl.CostEstimate(flops=flops, bytes_accessed=moved, transcendentals=transcendentals)


def along(a, b):
    pairs = []
    for i in range(32):
        x, y, core = i // 8, i // 2 % 4, i % 2
        dx, dy = (a, b) if core == 0 else (b, a)
        pairs.append((i, (x + dx) % 4 * 8 + (y + dy) % 4 * 2 + core))
    return pairs


SWAP = [(i, i ^ 1) for i in range(32)]


def body(
    child_values,
    parent_values,
    child_logits,
    parent_logits,
    prior_logits,
    weights,
    block_cols,
    parent_map,
):
    f32, bf16, i32 = jnp.float32, jnp.bfloat16, jnp.int32
    shape = jax.ShapeDtypeStruct
    parts = lax.axis_size("batch")
    rows = BLK // parts
    weights = weights[:, 0]
    region = lax.axis_index("region").astype(i32)
    core = lax.rem(region, 2)
    x, y = lax.shift_right_logical(region, 3), lax.shift_right_logical(region, 1) & 3
    place = jnp.stack(
        [
            core,
            lax.axis_index("batch").astype(i32),
            jnp.where(core == 0, x, y),
            jnp.where(core == 0, y, x),
        ]
    )

    columns = block_cols[:, 0].T

    def scores(half):
        return pl.pallas_call(
            child_kernel,
            out_shape=shape((HALF + 1, S_LOC, BLK), bf16),
            in_specs=[SMEM, VMEM, VMEM],
            out_specs=VMEM,
            scratch_shapes=[pltpu.VMEM((HALF, S_LOC, BLK), f32)],
            compiler_params=params(16),
            cost_estimate=cost(1 << 27, 2 << 20, 1 << 20),
            name="child_scores",
        )(half.reshape(1), child_values.T, child_logits)

    given, other_columns = lax.optimization_barrier(
        (lax.ppermute(scores(1 - core), "region", SWAP), lax.ppermute(columns, "region", SWAP))
    )
    kept = scores(core)
    own = pl.pallas_call(
        pack_kernel,
        out_shape=shape((PIECE, S_LOC, BLK), bf16),
        in_specs=[SMEM, VMEM, VMEM],
        out_specs=VMEM,
        compiler_params=params(8),
        name="pack",
    )(place, kept, given)

    def send(value, a, b):
        return lax.ppermute(value, "region", along(a, b))

    parent_in = pl.pallas_call(
        parent_kernel,
        out_shape=shape((P_SIZE, S_LOC, BLK), f32),
        in_specs=[VMEM, VMEM, VMEM],
        out_specs=VMEM,
        compiler_params=params(12),
        cost_estimate=cost(1 << 28, 3 << 20, 1 << 21),
        name="parent_scores",
    )(parent_values.T, parent_logits, prior_logits)
    a1, a3, a2 = lax.optimization_barrier((send(own, 1, 0), send(own, -1, 0), send(own, 2, 0)))
    near = jnp.concatenate([own, a1])
    near_up, near_down = send(near, 0, 1), send(near, 0, -1)
    far = jnp.concatenate([a3, a2])
    far_up, far_down = send(far, 0, 1), send(far, 0, -1)
    near_up, far_down = lax.optimization_barrier((near_up, far_down))
    next_up = send(near_up, 0, 1)
    next_down = send(far_down, 0, -1)
    slots = shape((HALF * NZ + 1, S_LOC, BLK), bf16)
    for_other, pool, powers = pl.pallas_call(
        pick_other_kernel,
        out_shape=(
            slots,
            shape((16 * PIECE, S_LOC, BLK), bf16),
            shape((32, S_LOC, BLK), f32),
        ),
        in_specs=[SMEM, SMEM] + [VMEM] * len(PLACES),
        out_specs=(VMEM, VMEM, VMEM),
        compiler_params=params(22),
        cost_estimate=cost(1 << 22, 20 << 20, 1 << 20),
        name="pick_other",
    )(place, other_columns, near, far, near_up, far_up, near_down, far_down, next_up, next_down)
    other = lax.ppermute(for_other, "region", SWAP)
    half_sums = shape((HALF, S_LOC, BLK), f32)
    scores_all = shape((P_SIZE, S_LOC, BLK), f32)
    picked, own_sums, own_root = pl.pallas_call(
        own_sums_kernel,
        out_shape=(shape((HALF * NZ, S_LOC, BLK), bf16), half_sums, scores_all),
        in_specs=[SMEM, SMEM, SMEM] + [VMEM] * 4,
        out_specs=(VMEM,) * 3,
        compiler_params=params(20),
        cost_estimate=cost(1 << 28, 8 << 20, 1 << 19),
        name="own_sums",
    )(place, columns, parent_map, pool, powers, weights, parent_in)
    stats, root, other_sums = pl.pallas_call(
        sums_kernel,
        out_shape=(shape((S_LOC, BLK), f32), scores_all, half_sums),
        in_specs=[SMEM, SMEM] + [VMEM] * 4,
        out_specs=(VMEM,) * 3,
        compiler_params=params(16),
        cost_estimate=cost(1 << 28, 8 << 20, 1 << 20),
        name="row_sums",
    )(place, parent_map, other, weights, own_root, prior_logits)

    for axis, pairs in (
        ("core", (SWAP,)),
        ("a", tuple(along(step, 0) for step in (1, 3, 2))),
        ("b", tuple(along(0, step) for step in (1, 3, 2))),
    ):
        others = [lax.ppermute(stats, "region", p) for p in pairs]
        if axis == "b":
            break
        stats = pl.pallas_call(
            merge_kernel,
            out_shape=shape((S_LOC, BLK), f32),
            in_specs=[VMEM] * (1 + len(others)),
            out_specs=VMEM,
            compiler_params=params(4),
            name="merge_" + axis,
        )(stats, *others)
    scale = K * NZ * BLK / (S_LOC * parts)
    whole, half_set = shape((C, NZ, rows, BLK), bf16), shape((HALF, NZ, rows, BLK), bf16)
    n0, n1, n2, n3, n5, n6, n7, far_up, far_down, loglik = pl.pallas_call(
        lambda *refs: counts_kernel(scale, 1 + len(others), *refs),
        out_shape=(whole,) * 7 + (half_set,) * 2 + (shape((S_LOC, BLK), f32),),
        in_specs=[SMEM, SMEM] + [VMEM] * (7 + len(others)),
        out_specs=(VMEM,) * 10,
        scratch_shapes=[pltpu.VMEM((P_SIZE, S_LOC, BLK), bf16)],
        compiler_params=params(24),
        cost_estimate=cost(1 << 29, 13 << 20, 1 << 19),
        name="counts",
    )(place, parent_map, stats, *others, root, own_sums, other_sums, picked, other, weights)

    def ring(up, down):
        shift = lambda step: [(i, (i + step) % parts) for i in range(parts)]
        return lax.ppermute(up, "batch", shift(1)), lax.ppermute(down, "batch", shift(-1))

    up, down = ring(far_up, far_down)
    for kernel, here_up, here_down in (
        (first_step_kernel, n3, n5),
        (step_kernel, n2, n6),
        (step_kernel, n1, n7),
    ):
        up, down = ring(
            *pl.pallas_call(
                kernel,
                out_shape=(whole, whole),
                in_specs=[VMEM] * 4,
                out_specs=(VMEM, VMEM),
                compiler_params=params(8),
                name="ring_add",
            )(here_up, here_down, up, down)
        )
    counts = pl.pallas_call(
        last_kernel,
        out_shape=whole,
        in_specs=[SMEM] + [VMEM] * 3,
        out_specs=VMEM,
        compiler_params=params(8),
        name="ring_last",
    )(place, n0, up, down)
    return (counts[:, None], loglik[:, 0])


def solution(mesh):
    return jax.shard_map(
        body,
        mesh=mesh,
        in_specs=(
            P("batch", None),
            P("batch", None),
            P(None, None, "region"),
            P(None, None, "region"),
            P(None, "region"),
            P(None, "region", None, None, None),
            P(None, "region", None),
            P(),
        ),
        out_specs=(P(None, "region", None, "batch", None), P("batch")),
        check_vma=False,
    )
```

```python
import jax
import jax.numpy as jnp
from jax import lax
from jax.experimental import pallas as pl
from jax.experimental.pallas import tpu as pltpu
from jax.sharding import PartitionSpec as P

K = 4096
BLK = 128
NZ = 4
C = 32
P_SIZE = 32
S_LOC = 64
LN2 = 0.6931471805599453
LOG2E = 1.4426950408889634
HALF = C // 2
PIECE = 2 * HALF + 1
VMEM = pl.BlockSpec(memory_space=pltpu.VMEM)
SMEM = pl.BlockSpec(memory_space=pltpu.SMEM)
ANY = pl.BlockSpec(memory_space=pl.ANY)


def lane_of(shape):
    return lax.broadcasted_iota(jnp.int32, shape, len(shape) - 1)


def look_up(values, table):
    wide = table.astype(jnp.float32)
    top = jnp.max(wide, axis=0, keepdims=True)
    log_norm = jnp.log(jnp.sum(jnp.exp(wide - top), axis=0, keepdims=True)) + top
    hot = (values == lane_of((S_LOC, table.shape[0]))).astype(jnp.float32)
    looked = jnp.dot(hot.astype(jnp.bfloat16), table, preferred_element_type=jnp.float32)
    return looked - log_norm


def child_kernel(half_ref, values_ref, table_ref, out_ref, inputs):
    half = half_ref[0]
    values = values_ref[...].T
    values = jnp.where(half == 0, values[:, :HALF], values[:, HALF:])
    for k in range(HALF):
        inputs[k] = look_up(values[:, k : k + 1], table_ref[half * HALF + k])
    powers = jnp.zeros((S_LOC, BLK), jnp.float32)
    lanes = lane_of((S_LOC, BLK))
    for k in range(HALF):
        powers = jnp.where(lanes == k, jnp.max(inputs[k], axis=1, keepdims=True), powers)
    powers = jnp.ceil(powers * LOG2E).astype(jnp.bfloat16)
    out_ref[HALF] = powers
    powers = powers.astype(jnp.float32) * LN2
    for k in range(HALF):
        out_ref[k] = jnp.exp(inputs[k] - powers[:, k : k + 1]).astype(jnp.bfloat16)


def pack_kernel(core_ref, own_ref, other_ref, out_ref):
    core = core_ref[0]
    out_ref[pl.ds(core * HALF, HALF)] = own_ref[:HALF]
    out_ref[pl.ds((1 - core) * HALF, HALF)] = other_ref[:HALF]
    own = own_ref[HALF].astype(jnp.float32)
    other = other_ref[HALF].astype(jnp.float32)
    low = jnp.where(core == 0, own, other)
    high = jnp.where(core == 0, other, own)
    powers = jnp.where(lane_of((S_LOC, BLK)) < HALF, low, pltpu.roll(high, HALF, 1))
    out_ref[2 * HALF] = powers.astype(jnp.bfloat16)


def parent_kernel(values_ref, table_ref, prior_ref, out_ref):
    values = values_ref[...].T
    for p in range(P_SIZE):
        out_ref[p] = look_up(values[:, p : p + 1], table_ref[p]) + prior_ref[p : p + 1, :]


PLACES = (
    ((0, 0), (3, 0)),
    ((1, 0), (2, 0)),
    ((0, 3), (3, 3)),
    ((1, 3), (2, 3)),
    ((0, 1), (3, 1)),
    ((1, 1), (2, 1)),
    ((0, 2),),
    ((3, 2),),
    ((1, 2),),
    ((2, 2),),
)


def codes_of(place_ref, columns_ref, k):
    core = place_ref[0]
    codes = []
    for z in range(NZ):
        column = columns_ref[z, core * HALF + k]
        x, y = lax.shift_right_logical(column, 3), lax.shift_right_logical(column, 1) & 3
        a = (jnp.where(core == 0, x, y) - place_ref[2]) & 3
        b = (jnp.where(core == 0, y, x) - place_ref[3]) & 3
        codes.append((a * 4 + b) * 2 + (column & 1))
    return codes


def pick_child(codes, k, pool, powers):
    power = [powers[code][:, k : k + 1] for code in codes]
    top = jnp.maximum(jnp.maximum(power[0], power[1]), jnp.maximum(power[2], power[3]))
    blocks = []
    for code, mine in zip(codes, power):
        factor = jnp.broadcast_to(jnp.exp2(mine - top), (S_LOC, BLK))
        block = pool[lax.shift_right_logical(code, 1) * PIECE + (code & 1) * HALF + k]
        blocks.append((block.astype(jnp.float32) * factor).astype(jnp.bfloat16))
    return blocks, top


def pick_other_kernel(place_ref, columns_ref, *refs):
    sources, (out_ref, pool, powers) = refs[: len(PLACES)], refs[len(PLACES) :]

    def collect(k, carry):
        for source, places in zip(sources, PLACES):
            for n, (a, b) in enumerate(places):
                pool[(a * 4 + b) * PIECE + k] = source[n * PIECE + k]
        return carry

    lax.fori_loop(0, PIECE, collect, 0)
    for piece in range(16):
        both = pool[piece * PIECE + 2 * HALF].astype(jnp.float32)
        powers[2 * piece] = both
        powers[2 * piece + 1] = pltpu.roll(both, BLK - HALF, 1)
    lanes = lane_of((S_LOC, BLK))
    tops = jnp.zeros((S_LOC, BLK), jnp.float32)
    for k in range(HALF):
        blocks, top = pick_child(codes_of(place_ref, columns_ref, k), k, pool, powers)
        tops = jnp.where(lanes == k, top, tops)
        for z in range(NZ):
            out_ref[k * NZ + z] = blocks[z]
    out_ref[HALF * NZ] = tops.astype(jnp.bfloat16)


def row_sum(blocks, weights_ref, child):
    total = None
    for z in range(0, NZ, 2):
        picked = jnp.concatenate(blocks[z : z + 2], axis=1)
        wide = jnp.concatenate([weights_ref[child, z], weights_ref[child, z + 1]], axis=1)
        term = lax.dot_general(
            picked, wide, (((1,), (1,)), ((), ())), preferred_element_type=jnp.float32
        )
        total = term if total is None else total + term
    return total


def child_at(core, half, k):
    return jnp.where(core == half, k, HALF + k)


def own_sums_kernel(
    place_ref, columns_ref, map_ref, pool, powers, weights_ref, parent_ref,
    out_ref, sums_ref, root_ref,
):
    root_ref[...] = parent_ref[...]
    for k in range(HALF):
        child = child_at(place_ref[0], 0, k)
        blocks, top = pick_child(codes_of(place_ref, columns_ref, k), k, pool, powers)
        for z in range(NZ):
            out_ref[k * NZ + z] = blocks[z]
        row_sums = row_sum(blocks, weights_ref, child)
        sums_ref[k] = row_sums
        owner = map_ref[child]
        root_ref[owner] = root_ref[owner] + (jnp.log(row_sums) + top * LN2)


def sums_kernel(
    place_ref, map_ref, other_ref, weights_ref, own_root_ref, prior_ref,
    stats_ref, root_ref, sums_ref,
):
    root_ref[...] = own_root_ref[...]
    tops = other_ref[HALF * NZ].astype(jnp.float32) * LN2
    for k in range(HALF):
        child = child_at(place_ref[0], 1, k)
        row_sums = row_sum([other_ref[k * NZ + z] for z in range(NZ)], weights_ref, child)
        sums_ref[k] = row_sums
        owner = map_ref[child]
        root_ref[owner] = root_ref[owner] + (jnp.log(row_sums) + tops[:, k : k + 1])
    lanes = lane_of((S_LOC, BLK))
    prior = prior_ref[...]
    prior_peak = jnp.max(prior, axis=1, keepdims=True)
    prior_total = jnp.sum(jnp.exp(prior - prior_peak), axis=1, keepdims=True)
    eye = lax.broadcasted_iota(jnp.int32, (P_SIZE, BLK), 0)
    wide = lane_of((P_SIZE, BLK))
    stats = jnp.sum(
        jnp.where(wide == eye + 2 * P_SIZE, prior_peak, 0.0)
        + jnp.where(wide == eye + 3 * P_SIZE, prior_total, 0.0),
        axis=0, keepdims=True,
    )
    stats = jnp.broadcast_to(stats, (S_LOC, BLK))
    peaks = [jnp.max(root_ref[p], axis=1, keepdims=True) for p in range(P_SIZE)]
    for p in range(P_SIZE):
        total = jnp.sum(jnp.exp(root_ref[p] - peaks[p]), axis=1, keepdims=True)
        stats = jnp.where(lanes == p, peaks[p], stats)
        stats = jnp.where(lanes == P_SIZE + p, total, stats)
    stats_ref[...] = stats


def merge(stats):
    is_peak = lane_of((S_LOC, BLK)) % (2 * P_SIZE) < P_SIZE
    peaks = [jnp.where(is_peak, s, pltpu.roll(s, P_SIZE, 1)) for s in stats]
    best = peaks[0]
    for p in peaks[1:]:
        best = jnp.maximum(best, p)
    total = None
    for s, p in zip(stats, peaks):
        term = s * jnp.exp(p - best)
        total = term if total is None else total + term
    return jnp.where(is_peak, best, total)


def merge_kernel(*refs):
    refs[-1][...] = merge([r[...] for r in refs[:-1]])


def counts_kernel(scale, n_stats, place_ref, map_ref, *refs):
    stats_refs, refs = refs[:n_stats], refs[n_stats:]
    root_ref, own_sums_ref, other_sums_ref, own_ref, other_ref, weights_ref = refs[:6]
    near, far, loglik_ref, posterior = refs[6:13], refs[13:15], refs[15], refs[16]
    core, place = place_ref[0], place_ref[1]
    stats = merge([r[...] for r in stats_refs])
    lanes = lane_of((S_LOC, BLK))
    norm = stats + pltpu.roll(jnp.log(stats), BLK - P_SIZE, 1)
    signed = jnp.where(lanes < P_SIZE, norm, 0.0) - jnp.where(
        (lanes >= 2 * P_SIZE) & (lanes < 3 * P_SIZE), norm, 0.0
    )
    loglik = jnp.sum(signed, axis=1, keepdims=True) / (C + P_SIZE)
    loglik_ref[...] = jnp.broadcast_to(loglik, (S_LOC, BLK))
    for p in range(P_SIZE):
        posterior[p] = jnp.exp(root_ref[p] - norm[:, p : p + 1]).astype(jnp.bfloat16)
    rows = near[0].shape[2]
    parts = BLK // rows
    starts = [pl.multiple_of(lax.rem(place + k, parts) * rows, rows) for k in range(parts)]
    turn = lax.rem(parts - place, parts) * rows
    for half, (picked_ref, sums_ref) in enumerate(
        ((own_ref, own_sums_ref), (other_ref, other_sums_ref))
    ):
        for k in range(HALF):
            child = child_at(core, half, k)
            share = posterior[map_ref[child]].astype(jnp.float32) / sums_ref[k]
            share = pltpu.roll(share, turn, 1).astype(jnp.bfloat16)
            picked = jnp.concatenate([picked_ref[k * NZ + z] for z in range(NZ)], axis=1)
            flow = lax.dot_general(
                share, picked, (((0,), (0,)), ((), ())), preferred_element_type=jnp.float32
            )
            for distance in range(parts):
                for z in range(NZ):
                    weight = weights_ref[child, z, pl.ds(starts[distance], rows), :]
                    block = flow[distance * rows : (distance + 1) * rows, z * BLK : (z + 1) * BLK]
                    block = (block * (weight.astype(jnp.float32) * scale)).astype(jnp.bfloat16)
                    if distance == 4:
                        far[half][k, z] = block
                    else:
                        near[distance if distance < 4 else distance - 1][half * HALF + k, z] = block


def first_step_kernel(up_ref, down_ref, up_in_ref, down_in_ref, up_out_ref, down_out_ref):
    f32 = jnp.float32
    low, high = pl.ds(0, HALF), pl.ds(HALF, HALF)
    up_out_ref[low] = (up_ref[low].astype(f32) + up_in_ref[...].astype(f32)).astype(jnp.bfloat16)
    up_out_ref[high] = up_ref[high]
    down_out_ref[low] = down_ref[low]
    down_out_ref[high] = (down_ref[high].astype(f32) + down_in_ref[...].astype(f32)).astype(
        jnp.bfloat16
    )


def step_kernel(up_ref, down_ref, up_in_ref, down_in_ref, up_out_ref, down_out_ref):
    f32 = jnp.float32
    up_out_ref[...] = (up_ref[...].astype(f32) + up_in_ref[...].astype(f32)).astype(jnp.bfloat16)
    down_out_ref[...] = (down_ref[...].astype(f32) + down_in_ref[...].astype(f32)).astype(
        jnp.bfloat16
    )


def last_kernel(core_ref, own_ref, up_in_ref, down_in_ref, out_ref):
    f32 = jnp.float32
    core = core_ref[0]
    for half in range(2):
        part = pl.ds(half * HALF, HALF)
        total = own_ref[part].astype(f32) + up_in_ref[part].astype(f32) + down_in_ref[part].astype(f32)
        out_ref[pl.ds(jnp.where(core == half, 0, HALF), HALF)] = total.astype(jnp.bfloat16)


def params(mib):
    return pltpu.CompilerParams(vmem_limit_bytes=mib << 20)


def cost(flops, moved, transcendentals):
    return pl.CostEstimate(flops=flops, bytes_accessed=moved, transcendentals=transcendentals)


def along(a, b):
    pairs = []
    for i in range(32):
        x, y, core = i // 8, i // 2 % 4, i % 2
        dx, dy = (a, b) if core == 0 else (b, a)
        pairs.append((i, (x + dx) % 4 * 8 + (y + dy) % 4 * 2 + core))
    return pairs


SWAP = [(i, i ^ 1) for i in range(32)]


def body(
    child_values,
    parent_values,
    child_logits,
    parent_logits,
    prior_logits,
    weights,
    block_cols,
    parent_map,
):
    f32, bf16, i32 = jnp.float32, jnp.bfloat16, jnp.int32
    shape = jax.ShapeDtypeStruct
    parts = lax.axis_size("batch")
    rows = BLK // parts
    weights = weights[:, 0]
    region = lax.axis_index("region").astype(i32)
    core = lax.rem(region, 2)
    x, y = lax.shift_right_logical(region, 3), lax.shift_right_logical(region, 1) & 3
    place = jnp.stack(
        [
            core,
            lax.axis_index("batch").astype(i32),
            jnp.where(core == 0, x, y),
            jnp.where(core == 0, y, x),
        ]
    )

    columns = block_cols[:, 0].T

    def scores(half):
        return pl.pallas_call(
            child_kernel,
            out_shape=shape((HALF + 1, S_LOC, BLK), bf16),
            in_specs=[SMEM, VMEM, VMEM],
            out_specs=VMEM,
            scratch_shapes=[pltpu.VMEM((HALF, S_LOC, BLK), f32)],
            compiler_params=params(16),
            cost_estimate=cost(1 << 27, 2 << 20, 1 << 20),
            name="child_scores",
        )(half.reshape(1), child_values.T, child_logits)

    given, other_columns = lax.optimization_barrier(
        (lax.ppermute(scores(1 - core), "region", SWAP), lax.ppermute(columns, "region", SWAP))
    )
    kept = scores(core)
    own = pl.pallas_call(
        pack_kernel,
        out_shape=shape((PIECE, S_LOC, BLK), bf16),
        in_specs=[SMEM, VMEM, VMEM],
        out_specs=VMEM,
        compiler_params=params(8),
        name="pack",
    )(place, kept, given)

    def send(value, a, b):
        return lax.ppermute(value, "region", along(a, b))

    parent_in = pl.pallas_call(
        parent_kernel,
        out_shape=shape((P_SIZE, S_LOC, BLK), f32),
        in_specs=[VMEM, VMEM, VMEM],
        out_specs=VMEM,
        compiler_params=params(12),
        cost_estimate=cost(1 << 28, 3 << 20, 1 << 21),
        name="parent_scores",
    )(parent_values.T, parent_logits, prior_logits)
    cut = (PIECE + 1) // 2
    a1, a3 = lax.optimization_barrier((send(own, 1, 0), send(own, -1, 0)))
    c1, c3 = send(a1[:cut], 1, 0), send(a3[cut:], -1, 0)
    near = jnp.concatenate([own, a1])
    near_up, near_down = send(near, 0, 1), send(near, 0, -1)
    c1, c3 = lax.optimization_barrier((c1, c3))
    far = jnp.concatenate([a3, c1, c3])
    far_up, far_down = send(far, 0, 1), send(far, 0, -1)
    near_up, near_down = lax.optimization_barrier((near_up, near_down))
    next_up, next_down = send(near_up[:PIECE], 0, 1), send(near_down[PIECE:], 0, -1)
    far_up, far_down, near_down = lax.optimization_barrier((far_up, far_down, near_down))
    last_up, last_down = send(far_up[:PIECE], 0, 1), send(far_down[PIECE:], 0, -1)
    slots = shape((HALF * NZ + 1, S_LOC, BLK), bf16)
    for_other, pool, powers = pl.pallas_call(
        pick_other_kernel,
        out_shape=(
            slots,
            shape((16 * PIECE, S_LOC, BLK), bf16),
            shape((32, S_LOC, BLK), f32),
        ),
        in_specs=[SMEM, SMEM] + [VMEM] * len(PLACES),
        out_specs=(VMEM, VMEM, VMEM),
        compiler_params=params(22),
        cost_estimate=cost(1 << 22, 20 << 20, 1 << 20),
        name="pick_other",
    )(place, other_columns, near, far, near_up, far_up, near_down, far_down, next_up, next_down, last_up, last_down)
    other = lax.ppermute(for_other, "region", SWAP)
    half_sums = shape((HALF, S_LOC, BLK), f32)
    scores_all = shape((P_SIZE, S_LOC, BLK), f32)
    picked, own_sums, own_root = pl.pallas_call(
        own_sums_kernel,
        out_shape=(shape((HALF * NZ, S_LOC, BLK), bf16), half_sums, scores_all),
        in_specs=[SMEM, SMEM, SMEM] + [VMEM] * 4,
        out_specs=(VMEM,) * 3,
        compiler_params=params(20),
        cost_estimate=cost(1 << 28, 8 << 20, 1 << 19),
        name="own_sums",
    )(place, columns, parent_map, pool, powers, weights, parent_in)
    stats, root, other_sums = pl.pallas_call(
        sums_kernel,
        out_shape=(shape((S_LOC, BLK), f32), scores_all, half_sums),
        in_specs=[SMEM, SMEM] + [VMEM] * 4,
        out_specs=(VMEM,) * 3,
        compiler_params=params(16),
        cost_estimate=cost(1 << 28, 8 << 20, 1 << 20),
        name="row_sums",
    )(place, parent_map, other, weights, own_root, prior_logits)

    for axis, pairs in (
        ("core", (SWAP,)),
        ("a", tuple(along(step, 0) for step in (1, 3, 2))),
        ("b", tuple(along(0, step) for step in (1, 3, 2))),
    ):
        others = [lax.ppermute(stats, "region", p) for p in pairs]
        if axis == "b":
            break
        stats = pl.pallas_call(
            merge_kernel,
            out_shape=shape((S_LOC, BLK), f32),
            in_specs=[VMEM] * (1 + len(others)),
            out_specs=VMEM,
            compiler_params=params(4),
            name="merge_" + axis,
        )(stats, *others)
    scale = K * NZ * BLK / (S_LOC * parts)
    whole, half_set = shape((C, NZ, rows, BLK), bf16), shape((HALF, NZ, rows, BLK), bf16)
    n0, n1, n2, n3, n5, n6, n7, far_up, far_down, loglik = pl.pallas_call(
        lambda *refs: counts_kernel(scale, 1 + len(others), *refs),
        out_shape=(whole,) * 7 + (half_set,) * 2 + (shape((S_LOC, BLK), f32),),
        in_specs=[SMEM, SMEM] + [VMEM] * (7 + len(others)),
        out_specs=(VMEM,) * 10,
        scratch_shapes=[pltpu.VMEM((P_SIZE, S_LOC, BLK), bf16)],
        compiler_params=params(24),
        cost_estimate=cost(1 << 29, 13 << 20, 1 << 19),
        name="counts",
    )(place, parent_map, stats, *others, root, own_sums, other_sums, picked, other, weights)

    def ring(up, down):
        shift = lambda step: [(i, (i + step) % parts) for i in range(parts)]
        return lax.ppermute(up, "batch", shift(1)), lax.ppermute(down, "batch", shift(-1))

    up, down = ring(far_up, far_down)
    for kernel, here_up, here_down in (
        (first_step_kernel, n3, n5),
        (step_kernel, n2, n6),
        (step_kernel, n1, n7),
    ):
        up, down = ring(
            *pl.pallas_call(
                kernel,
                out_shape=(whole, whole),
                in_specs=[VMEM] * 4,
                out_specs=(VMEM, VMEM),
                compiler_params=params(8),
                name="ring_add",
            )(here_up, here_down, up, down)
        )
    counts = pl.pallas_call(
        last_kernel,
        out_shape=whole,
        in_specs=[SMEM] + [VMEM] * 3,
        out_specs=VMEM,
        compiler_params=params(8),
        name="ring_last",
    )(place, n0, up, down)
    return (counts[:, None], loglik[:, 0])


def solution(mesh):
    return jax.shard_map(
        body,
        mesh=mesh,
        in_specs=(
            P("batch", None),
            P("batch", None),
            P(None, None, "region"),
            P(None, None, "region"),
            P(None, "region"),
            P(None, "region", None, None, None),
            P(None, "region", None),
            P(),
        ),
        out_specs=(P(None, "region", None, "batch", None), P("batch")),
        check_vma=False,
    )
```

```python
import jax
import jax.numpy as jnp
from jax import lax
from jax.experimental import pallas as pl
from jax.experimental.pallas import tpu as pltpu
from jax.sharding import PartitionSpec as P

K = 4096
BLK = 128
NZ = 4
C = 32
P_SIZE = 32
S_LOC = 64
LN2 = 0.6931471805599453
LOG2E = 1.4426950408889634
HALF = C // 2
PIECE = 2 * HALF + 1
VMEM = pl.BlockSpec(memory_space=pltpu.VMEM)
SMEM = pl.BlockSpec(memory_space=pltpu.SMEM)
ANY = pl.BlockSpec(memory_space=pl.ANY)


def lane_of(shape):
    return lax.broadcasted_iota(jnp.int32, shape, len(shape) - 1)


def look_up(values, table):
    wide = table.astype(jnp.float32)
    top = jnp.max(wide, axis=0, keepdims=True)
    log_norm = jnp.log(jnp.sum(jnp.exp(wide - top), axis=0, keepdims=True)) + top
    hot = (values == lane_of((S_LOC, table.shape[0]))).astype(jnp.float32)
    looked = jnp.dot(hot.astype(jnp.bfloat16), table, preferred_element_type=jnp.float32)
    return looked - log_norm


def child_kernel(half_ref, values_ref, table_ref, out_ref, inputs):
    half = half_ref[0]
    values = values_ref[...].T
    values = jnp.where(half == 0, values[:, :HALF], values[:, HALF:])
    for k in range(HALF):
        inputs[k] = look_up(values[:, k : k + 1], table_ref[half * HALF + k])
    powers = jnp.zeros((S_LOC, BLK), jnp.float32)
    lanes = lane_of((S_LOC, BLK))
    for k in range(HALF):
        powers = jnp.where(lanes == k, jnp.max(inputs[k], axis=1, keepdims=True), powers)
    powers = jnp.ceil(powers * LOG2E).astype(jnp.bfloat16)
    out_ref[HALF] = powers
    powers = powers.astype(jnp.float32) * LN2
    for k in range(HALF):
        out_ref[k] = jnp.exp(inputs[k] - powers[:, k : k + 1]).astype(jnp.bfloat16)


def pack_kernel(core_ref, own_ref, other_ref, out_ref):
    core = core_ref[0]
    out_ref[pl.ds(core * HALF, HALF)] = own_ref[:HALF]
    out_ref[pl.ds((1 - core) * HALF, HALF)] = other_ref[:HALF]
    own = own_ref[HALF].astype(jnp.float32)
    other = other_ref[HALF].astype(jnp.float32)
    low = jnp.where(core == 0, own, other)
    high = jnp.where(core == 0, other, own)
    powers = jnp.where(lane_of((S_LOC, BLK)) < HALF, low, pltpu.roll(high, HALF, 1))
    out_ref[2 * HALF] = powers.astype(jnp.bfloat16)


def parent_kernel(values_ref, table_ref, prior_ref, out_ref):
    values = values_ref[...].T
    for p in range(P_SIZE):
        out_ref[p] = look_up(values[:, p : p + 1], table_ref[p]) + prior_ref[p : p + 1, :]


PLACES = (
    ((0, 0), (3, 0)),
    ((1, 0), (2, 0)),
    ((0, 3), (3, 3)),
    ((1, 3), (2, 3)),
    ((0, 1), (3, 1)),
    ((1, 1), (2, 1)),
    ((0, 2),),
    ((3, 2),),
    ((1, 2),),
    ((2, 2),),
)


def codes_of(place_ref, columns_ref, k):
    core = place_ref[0]
    codes = []
    for z in range(NZ):
        column = columns_ref[z, core * HALF + k]
        x, y = lax.shift_right_logical(column, 3), lax.shift_right_logical(column, 1) & 3
        a = (jnp.where(core == 0, x, y) - place_ref[2]) & 3
        b = (jnp.where(core == 0, y, x) - place_ref[3]) & 3
        codes.append((a * 4 + b) * 2 + (column & 1))
    return codes


def pick_child(codes, k, pool, powers):
    power = [powers[code][:, k : k + 1] for code in codes]
    top = jnp.maximum(jnp.maximum(power[0], power[1]), jnp.maximum(power[2], power[3]))
    blocks = []
    for code, mine in zip(codes, power):
        factor = jnp.broadcast_to(jnp.exp2(mine - top), (S_LOC, BLK))
        block = pool[lax.shift_right_logical(code, 1) * PIECE + (code & 1) * HALF + k]
        blocks.append((block.astype(jnp.float32) * factor).astype(jnp.bfloat16))
    return blocks, top


def pick_other_kernel(place_ref, columns_ref, *refs):
    sources, (out_ref, pool, powers) = refs[: len(PLACES)], refs[len(PLACES) :]

    def collect(k, carry):
        for source, places in zip(sources, PLACES):
            for n, (a, b) in enumerate(places):
                pool[(a * 4 + b) * PIECE + k] = source[n * PIECE + k]
        return carry

    lax.fori_loop(0, PIECE, collect, 0)
    for piece in range(16):
        both = pool[piece * PIECE + 2 * HALF].astype(jnp.float32)
        powers[2 * piece] = both
        powers[2 * piece + 1] = pltpu.roll(both, BLK - HALF, 1)
    lanes = lane_of((S_LOC, BLK))
    tops = jnp.zeros((S_LOC, BLK), jnp.float32)
    for k in range(HALF):
        blocks, top = pick_child(codes_of(place_ref, columns_ref, k), k, pool, powers)
        tops = jnp.where(lanes == k, top, tops)
        for z in range(NZ):
            out_ref[k * NZ + z] = blocks[z]
    out_ref[HALF * NZ] = tops.astype(jnp.bfloat16)


def row_sum(blocks, weights_ref, child):
    total = None
    for z in range(0, NZ, 2):
        picked = jnp.concatenate(blocks[z : z + 2], axis=1)
        wide = jnp.concatenate([weights_ref[child, z], weights_ref[child, z + 1]], axis=1)
        term = lax.dot_general(
            picked, wide, (((1,), (1,)), ((), ())), preferred_element_type=jnp.float32
        )
        total = term if total is None else total + term
    return total


def child_at(core, half, k):
    return jnp.where(core == half, k, HALF + k)


def own_sums_kernel(
    place_ref, columns_ref, map_ref, pool, powers, weights_ref, parent_ref,
    out_ref, sums_ref, root_ref,
):
    root_ref[...] = parent_ref[...]
    for k in range(HALF):
        child = child_at(place_ref[0], 0, k)
        blocks, top = pick_child(codes_of(place_ref, columns_ref, k), k, pool, powers)
        for z in range(NZ):
            out_ref[k * NZ + z] = blocks[z]
        row_sums = row_sum(blocks, weights_ref, child)
        sums_ref[k] = row_sums
        owner = map_ref[child]
        root_ref[owner] = root_ref[owner] + (jnp.log(row_sums) + top * LN2)


def sums_kernel(
    place_ref, map_ref, other_ref, weights_ref, own_root_ref, prior_ref,
    stats_ref, root_ref, sums_ref,
):
    root_ref[...] = own_root_ref[...]
    tops = other_ref[HALF * NZ].astype(jnp.float32) * LN2
    for k in range(HALF):
        child = child_at(place_ref[0], 1, k)
        row_sums = row_sum([other_ref[k * NZ + z] for z in range(NZ)], weights_ref, child)
        sums_ref[k] = row_sums
        owner = map_ref[child]
        root_ref[owner] = root_ref[owner] + (jnp.log(row_sums) + tops[:, k : k + 1])
    lanes = lane_of((S_LOC, BLK))
    prior = prior_ref[...]
    prior_peak = jnp.max(prior, axis=1, keepdims=True)
    prior_total = jnp.sum(jnp.exp(prior - prior_peak), axis=1, keepdims=True)
    eye = lax.broadcasted_iota(jnp.int32, (P_SIZE, BLK), 0)
    wide = lane_of((P_SIZE, BLK))
    stats = jnp.sum(
        jnp.where(wide == eye + 2 * P_SIZE, prior_peak, 0.0)
        + jnp.where(wide == eye + 3 * P_SIZE, prior_total, 0.0),
        axis=0, keepdims=True,
    )
    stats = jnp.broadcast_to(stats, (S_LOC, BLK))
    peaks = [jnp.max(root_ref[p], axis=1, keepdims=True) for p in range(P_SIZE)]
    for p in range(P_SIZE):
        total = jnp.sum(jnp.exp(root_ref[p] - peaks[p]), axis=1, keepdims=True)
        stats = jnp.where(lanes == p, peaks[p], stats)
        stats = jnp.where(lanes == P_SIZE + p, total, stats)
    stats_ref[...] = stats


def merge(stats):
    is_peak = lane_of((S_LOC, BLK)) % (2 * P_SIZE) < P_SIZE
    peaks = [jnp.where(is_peak, s, pltpu.roll(s, P_SIZE, 1)) for s in stats]
    best = peaks[0]
    for p in peaks[1:]:
        best = jnp.maximum(best, p)
    total = None
    for s, p in zip(stats, peaks):
        term = s * jnp.exp(p - best)
        total = term if total is None else total + term
    return jnp.where(is_peak, best, total)


def merge_kernel(*refs):
    refs[-1][...] = merge([r[...] for r in refs[:-1]])


def counts_kernel(scale, place_ref, map_ref, stats_ref, *refs):
    root_ref, own_sums_ref, other_sums_ref, own_ref, other_ref, weights_ref = refs[:6]
    near, far, loglik_ref, posterior = refs[6:13], refs[13:15], refs[15], refs[16]
    core, place = place_ref[0], place_ref[1]
    stats = merge([stats_ref[i] for i in range(stats_ref.shape[0])])
    lanes = lane_of((S_LOC, BLK))
    norm = stats + pltpu.roll(jnp.log(stats), BLK - P_SIZE, 1)
    signed = jnp.where(lanes < P_SIZE, norm, 0.0) - jnp.where(
        (lanes >= 2 * P_SIZE) & (lanes < 3 * P_SIZE), norm, 0.0
    )
    loglik = jnp.sum(signed, axis=1, keepdims=True) / (C + P_SIZE)
    loglik_ref[...] = jnp.broadcast_to(loglik, (S_LOC, BLK))
    for p in range(P_SIZE):
        posterior[p] = jnp.exp(root_ref[p] - norm[:, p : p + 1]).astype(jnp.bfloat16)
    rows = near[0].shape[2]
    parts = BLK // rows
    starts = [pl.multiple_of(lax.rem(place + k, parts) * rows, rows) for k in range(parts)]
    turn = lax.rem(parts - place, parts) * rows
    for half, (picked_ref, sums_ref) in enumerate(
        ((own_ref, own_sums_ref), (other_ref, other_sums_ref))
    ):
        for k in range(HALF):
            child = child_at(core, half, k)
            share = posterior[map_ref[child]].astype(jnp.float32) / sums_ref[k]
            share = pltpu.roll(share, turn, 1).astype(jnp.bfloat16)
            picked = jnp.concatenate([picked_ref[k * NZ + z] for z in range(NZ)], axis=1)
            flow = lax.dot_general(
                share, picked, (((0,), (0,)), ((), ())), preferred_element_type=jnp.float32
            )
            for distance in range(parts):
                for z in range(NZ):
                    weight = weights_ref[child, z, pl.ds(starts[distance], rows), :]
                    block = flow[distance * rows : (distance + 1) * rows, z * BLK : (z + 1) * BLK]
                    block = (block * (weight.astype(jnp.float32) * scale)).astype(jnp.bfloat16)
                    if distance == 4:
                        far[half][k, z] = block
                    else:
                        near[distance if distance < 4 else distance - 1][half * HALF + k, z] = block


def first_step_kernel(up_ref, down_ref, up_in_ref, down_in_ref, up_out_ref, down_out_ref):
    f32 = jnp.float32
    low, high = pl.ds(0, HALF), pl.ds(HALF, HALF)
    up_out_ref[low] = (up_ref[low].astype(f32) + up_in_ref[...].astype(f32)).astype(jnp.bfloat16)
    up_out_ref[high] = up_ref[high]
    down_out_ref[low] = down_ref[low]
    down_out_ref[high] = (down_ref[high].astype(f32) + down_in_ref[...].astype(f32)).astype(
        jnp.bfloat16
    )


def step_kernel(up_ref, down_ref, up_in_ref, down_in_ref, up_out_ref, down_out_ref):
    f32 = jnp.float32
    up_out_ref[...] = (up_ref[...].astype(f32) + up_in_ref[...].astype(f32)).astype(jnp.bfloat16)
    down_out_ref[...] = (down_ref[...].astype(f32) + down_in_ref[...].astype(f32)).astype(
        jnp.bfloat16
    )


def last_kernel(core_ref, own_ref, up_in_ref, down_in_ref, out_ref):
    f32 = jnp.float32
    core = core_ref[0]
    for half in range(2):
        part = pl.ds(half * HALF, HALF)
        total = own_ref[part].astype(f32) + up_in_ref[part].astype(f32) + down_in_ref[part].astype(f32)
        out_ref[pl.ds(jnp.where(core == half, 0, HALF), HALF)] = total.astype(jnp.bfloat16)


def params(mib):
    return pltpu.CompilerParams(vmem_limit_bytes=mib << 20)


def cost(flops, moved, transcendentals):
    return pl.CostEstimate(flops=flops, bytes_accessed=moved, transcendentals=transcendentals)


def along(a, b):
    pairs = []
    for i in range(32):
        x, y, core = i // 8, i // 2 % 4, i % 2
        dx, dy = (a, b) if core == 0 else (b, a)
        pairs.append((i, (x + dx) % 4 * 8 + (y + dy) % 4 * 2 + core))
    return pairs


SWAP = [(i, i ^ 1) for i in range(32)]


def body(
    child_values,
    parent_values,
    child_logits,
    parent_logits,
    prior_logits,
    weights,
    block_cols,
    parent_map,
):
    f32, bf16, i32 = jnp.float32, jnp.bfloat16, jnp.int32
    shape = jax.ShapeDtypeStruct
    parts = lax.axis_size("batch")
    rows = BLK // parts
    weights = weights[:, 0]
    region = lax.axis_index("region").astype(i32)
    core = lax.rem(region, 2)
    x, y = lax.shift_right_logical(region, 3), lax.shift_right_logical(region, 1) & 3
    place = jnp.stack(
        [
            core,
            lax.axis_index("batch").astype(i32),
            jnp.where(core == 0, x, y),
            jnp.where(core == 0, y, x),
        ]
    )

    columns = block_cols[:, 0].T

    def scores(half):
        return pl.pallas_call(
            child_kernel,
            out_shape=shape((HALF + 1, S_LOC, BLK), bf16),
            in_specs=[SMEM, VMEM, VMEM],
            out_specs=VMEM,
            scratch_shapes=[pltpu.VMEM((HALF, S_LOC, BLK), f32)],
            compiler_params=params(16),
            cost_estimate=cost(1 << 27, 2 << 20, 1 << 20),
            name="child_scores",
        )(half.reshape(1), child_values.T, child_logits)

    given, other_columns = lax.optimization_barrier(
        (lax.ppermute(scores(1 - core), "region", SWAP), lax.ppermute(columns, "region", SWAP))
    )
    kept = scores(core)
    own = pl.pallas_call(
        pack_kernel,
        out_shape=shape((PIECE, S_LOC, BLK), bf16),
        in_specs=[SMEM, VMEM, VMEM],
        out_specs=VMEM,
        compiler_params=params(8),
        name="pack",
    )(place, kept, given)

    def send(value, a, b):
        return lax.ppermute(value, "region", along(a, b))

    parent_in = pl.pallas_call(
        parent_kernel,
        out_shape=shape((P_SIZE, S_LOC, BLK), f32),
        in_specs=[VMEM, VMEM, VMEM],
        out_specs=VMEM,
        compiler_params=params(12),
        cost_estimate=cost(1 << 28, 3 << 20, 1 << 21),
        name="parent_scores",
    )(parent_values.T, parent_logits, prior_logits)
    cut = (PIECE + 1) // 2
    a1, a3 = lax.optimization_barrier((send(own, 1, 0), send(own, -1, 0)))
    c1, c3 = send(a1[:cut], 1, 0), send(a3[cut:], -1, 0)
    near = jnp.concatenate([own, a1])
    near_up, near_down = send(near, 0, 1), send(near, 0, -1)
    c1, c3 = lax.optimization_barrier((c1, c3))
    far = jnp.concatenate([a3, c1, c3])
    far_up, far_down = send(far, 0, 1), send(far, 0, -1)
    near_up, near_down = lax.optimization_barrier((near_up, near_down))
    next_up, next_down = send(near_up[:PIECE], 0, 1), send(near_down[PIECE:], 0, -1)
    far_up, far_down, near_down = lax.optimization_barrier((far_up, far_down, near_down))
    last_up, last_down = send(far_up[:PIECE], 0, 1), send(far_down[PIECE:], 0, -1)
    slots = shape((HALF * NZ + 1, S_LOC, BLK), bf16)
    for_other, pool, powers = pl.pallas_call(
        pick_other_kernel,
        out_shape=(
            slots,
            shape((16 * PIECE, S_LOC, BLK), bf16),
            shape((32, S_LOC, BLK), f32),
        ),
        in_specs=[SMEM, SMEM] + [VMEM] * len(PLACES),
        out_specs=(VMEM, VMEM, VMEM),
        compiler_params=params(22),
        cost_estimate=cost(1 << 22, 20 << 20, 1 << 20),
        name="pick_other",
    )(place, other_columns, near, far, near_up, far_up, near_down, far_down, next_up, next_down, last_up, last_down)
    other = lax.ppermute(for_other, "region", SWAP)
    half_sums = shape((HALF, S_LOC, BLK), f32)
    scores_all = shape((P_SIZE, S_LOC, BLK), f32)
    picked, own_sums, own_root = pl.pallas_call(
        own_sums_kernel,
        out_shape=(shape((HALF * NZ, S_LOC, BLK), bf16), half_sums, scores_all),
        in_specs=[SMEM, SMEM, SMEM] + [VMEM] * 4,
        out_specs=(VMEM,) * 3,
        compiler_params=params(20),
        cost_estimate=cost(1 << 28, 8 << 20, 1 << 19),
        name="own_sums",
    )(place, columns, parent_map, pool, powers, weights, parent_in)
    stats, root, other_sums = pl.pallas_call(
        sums_kernel,
        out_shape=(shape((S_LOC, BLK), f32), scores_all, half_sums),
        in_specs=[SMEM, SMEM] + [VMEM] * 4,
        out_specs=(VMEM,) * 3,
        compiler_params=params(16),
        cost_estimate=cost(1 << 28, 8 << 20, 1 << 20),
        name="row_sums",
    )(place, parent_map, other, weights, own_root, prior_logits)

    def merged(name, *parts_of):
        return pl.pallas_call(
            merge_kernel,
            out_shape=shape((S_LOC, BLK), f32),
            in_specs=[VMEM] * len(parts_of),
            out_specs=VMEM,
            compiler_params=params(4),
            name=name,
        )(*parts_of)

    stats = merged("merge_core", stats, lax.ppermute(stats, "region", SWAP))
    same_core = [[2 * i + c for i in range(16)] for c in range(2)]
    others = [
        lax.all_to_all(
            jnp.broadcast_to(stats[None], (16, S_LOC, BLK)), "region", 0, 0, axis_index_groups=same_core
        )
    ]
    scale = K * NZ * BLK / (S_LOC * parts)
    whole, half_set = shape((C, NZ, rows, BLK), bf16), shape((HALF, NZ, rows, BLK), bf16)
    n0, n1, n2, n3, n5, n6, n7, far_up, far_down, loglik = pl.pallas_call(
        lambda *refs: counts_kernel(scale, *refs),
        out_shape=(whole,) * 7 + (half_set,) * 2 + (shape((S_LOC, BLK), f32),),
        in_specs=[SMEM, SMEM] + [VMEM] * 7,
        out_specs=(VMEM,) * 10,
        scratch_shapes=[pltpu.VMEM((P_SIZE, S_LOC, BLK), bf16)],
        compiler_params=params(24),
        cost_estimate=cost(1 << 29, 13 << 20, 1 << 19),
        name="counts",
    )(place, parent_map, *others, root, own_sums, other_sums, picked, other, weights)

    def ring(up, down):
        shift = lambda step: [(i, (i + step) % parts) for i in range(parts)]
        return lax.ppermute(up, "batch", shift(1)), lax.ppermute(down, "batch", shift(-1))

    up, down = ring(far_up, far_down)
    for kernel, here_up, here_down in (
        (first_step_kernel, n3, n5),
        (step_kernel, n2, n6),
        (step_kernel, n1, n7),
    ):
        up, down = ring(
            *pl.pallas_call(
                kernel,
                out_shape=(whole, whole),
                in_specs=[VMEM] * 4,
                out_specs=(VMEM, VMEM),
                compiler_params=params(8),
                name="ring_add",
            )(here_up, here_down, up, down)
        )
    counts = pl.pallas_call(
        last_kernel,
        out_shape=whole,
        in_specs=[SMEM] + [VMEM] * 3,
        out_specs=VMEM,
        compiler_params=params(8),
        name="ring_last",
    )(place, n0, up, down)
    return (counts[:, None], loglik[:, 0])


def solution(mesh):
    return jax.shard_map(
        body,
        mesh=mesh,
        in_specs=(
            P("batch", None),
            P("batch", None),
            P(None, None, "region"),
            P(None, None, "region"),
            P(None, "region"),
            P(None, "region", None, None, None),
            P(None, "region", None),
            P(),
        ),
        out_specs=(P(None, "region", None, "batch", None), P("batch")),
        check_vma=False,
    )
```

```python
import functools

import jax
import jax.numpy as jnp
from jax import lax
from jax.experimental import pallas as pl
from jax.experimental.pallas import tpu as pltpu
from jax.sharding import PartitionSpec as P

K = 4096
BLK = 128
NZ = 4
C = 32
P_SIZE = 32
S_LOC = 64
LN2 = 0.6931471805599453
LOG2E = 1.4426950408889634
HALF = C // 2
PIECE = 2 * HALF + 1
VMEM = pl.BlockSpec(memory_space=pltpu.VMEM)
SMEM = pl.BlockSpec(memory_space=pltpu.SMEM)
ANY = pl.BlockSpec(memory_space=pl.ANY)


def lane_of(shape):
    return lax.broadcasted_iota(jnp.int32, shape, len(shape) - 1)


def look_up(values, table):
    wide = table.astype(jnp.float32)
    top = jnp.max(wide, axis=0, keepdims=True)
    log_norm = jnp.log(jnp.sum(jnp.exp(wide - top), axis=0, keepdims=True)) + top
    hot = (values == lane_of((S_LOC, table.shape[0]))).astype(jnp.float32)
    looked = jnp.dot(hot.astype(jnp.bfloat16), table, preferred_element_type=jnp.float32)
    return looked - log_norm


def child_kernel(half_ref, values_ref, table_ref, out_ref, inputs):
    half = half_ref[0]
    values = values_ref[...].T
    values = jnp.where(half == 0, values[:, :HALF], values[:, HALF:])
    for k in range(HALF):
        inputs[k] = look_up(values[:, k : k + 1], table_ref[half * HALF + k])
    powers = jnp.zeros((S_LOC, BLK), jnp.float32)
    lanes = lane_of((S_LOC, BLK))
    for k in range(HALF):
        powers = jnp.where(lanes == k, jnp.max(inputs[k], axis=1, keepdims=True), powers)
    powers = jnp.ceil(powers * LOG2E).astype(jnp.bfloat16)
    out_ref[HALF] = powers
    powers = powers.astype(jnp.float32) * LN2
    for k in range(HALF):
        out_ref[k] = jnp.exp(inputs[k] - powers[:, k : k + 1]).astype(jnp.bfloat16)


def pack_kernel(core_ref, own_ref, other_ref, out_ref):
    core = core_ref[0]
    out_ref[pl.ds(core * HALF, HALF)] = own_ref[:HALF]
    out_ref[pl.ds((1 - core) * HALF, HALF)] = other_ref[:HALF]
    own = own_ref[HALF].astype(jnp.float32)
    other = other_ref[HALF].astype(jnp.float32)
    low = jnp.where(core == 0, own, other)
    high = jnp.where(core == 0, other, own)
    powers = jnp.where(lane_of((S_LOC, BLK)) < HALF, low, pltpu.roll(high, HALF, 1))
    out_ref[2 * HALF] = powers.astype(jnp.bfloat16)


def parent_kernel(values_ref, table_ref, prior_ref, out_ref):
    values = values_ref[...].T
    for p in range(P_SIZE):
        out_ref[p] = look_up(values[:, p : p + 1], table_ref[p]) + prior_ref[p : p + 1, :]


PLACES = (
    ((0, 0), (3, 0)),
    ((1, 0), (2, 0)),
    ((0, 3), (3, 3)),
    ((1, 3), (2, 3)),
    ((0, 1), (3, 1)),
    ((1, 1), (2, 1)),
    ((0, 2),),
    ((3, 2),),
    ((1, 2),),
    ((2, 2),),
)


def codes_of(place_ref, columns_ref, k):
    core = place_ref[0]
    codes = []
    for z in range(NZ):
        column = columns_ref[z, core * HALF + k]
        x, y = lax.shift_right_logical(column, 3), lax.shift_right_logical(column, 1) & 3
        a = (jnp.where(core == 0, x, y) - place_ref[2]) & 3
        b = (jnp.where(core == 0, y, x) - place_ref[3]) & 3
        codes.append((a * 4 + b) * 2 + (column & 1))
    return codes


def pick_child(codes, k, pool, powers):
    power = [powers[code][:, k : k + 1] for code in codes]
    top = jnp.maximum(jnp.maximum(power[0], power[1]), jnp.maximum(power[2], power[3]))
    blocks = []
    for code, mine in zip(codes, power):
        factor = jnp.broadcast_to(jnp.exp2(mine - top), (S_LOC, BLK))
        block = pool[lax.shift_right_logical(code, 1) * PIECE + (code & 1) * HALF + k]
        blocks.append((block.astype(jnp.float32) * factor).astype(jnp.bfloat16))
    return blocks, top


def pick_other_kernel(place_ref, columns_ref, *refs):
    sources, (out_ref, pool, powers) = refs[: len(PLACES)], refs[len(PLACES) :]

    def collect(k, carry):
        for source, places in zip(sources, PLACES):
            for n, (a, b) in enumerate(places):
                pool[(a * 4 + b) * PIECE + k] = source[n * PIECE + k]
        return carry

    lax.fori_loop(0, PIECE, collect, 0)
    for piece in range(16):
        both = pool[piece * PIECE + 2 * HALF].astype(jnp.float32)
        powers[2 * piece] = both
        powers[2 * piece + 1] = pltpu.roll(both, BLK - HALF, 1)
    lanes = lane_of((S_LOC, BLK))
    tops = jnp.zeros((S_LOC, BLK), jnp.float32)
    for k in range(HALF):
        blocks, top = pick_child(codes_of(place_ref, columns_ref, k), k, pool, powers)
        tops = jnp.where(lanes == k, top, tops)
        for z in range(NZ):
            out_ref[k * NZ + z] = blocks[z]
    out_ref[HALF * NZ] = tops.astype(jnp.bfloat16)


def row_sum(blocks, weights_ref, child):
    total = None
    for z in range(0, NZ, 2):
        picked = jnp.concatenate(blocks[z : z + 2], axis=1)
        wide = jnp.concatenate([weights_ref[child, z], weights_ref[child, z + 1]], axis=1)
        term = lax.dot_general(
            picked, wide, (((1,), (1,)), ((), ())), preferred_element_type=jnp.float32
        )
        total = term if total is None else total + term
    return total


def child_at(core, half, k):
    return jnp.where(core == half, k, HALF + k)


def own_sums_kernel(
    place_ref, columns_ref, map_ref, pool, powers, weights_ref, parent_ref,
    out_ref, sums_ref, root_ref,
):
    root_ref[...] = parent_ref[...]
    for k in range(HALF):
        child = child_at(place_ref[0], 0, k)
        blocks, top = pick_child(codes_of(place_ref, columns_ref, k), k, pool, powers)
        for z in range(NZ):
            out_ref[k * NZ + z] = blocks[z]
        row_sums = row_sum(blocks, weights_ref, child)
        sums_ref[k] = row_sums
        owner = map_ref[child]
        root_ref[owner] = root_ref[owner] + (jnp.log(row_sums) + top * LN2)


def sums_kernel(
    place_ref, map_ref, other_ref, weights_ref, own_root_ref, prior_ref,
    stats_ref, root_ref, sums_ref,
):
    root_ref[...] = own_root_ref[...]
    tops = other_ref[HALF * NZ].astype(jnp.float32) * LN2
    for k in range(HALF):
        child = child_at(place_ref[0], 1, k)
        row_sums = row_sum([other_ref[k * NZ + z] for z in range(NZ)], weights_ref, child)
        sums_ref[k] = row_sums
        owner = map_ref[child]
        root_ref[owner] = root_ref[owner] + (jnp.log(row_sums) + tops[:, k : k + 1])
    lanes = lane_of((S_LOC, BLK))
    prior = prior_ref[...]
    prior_peak = jnp.max(prior, axis=1, keepdims=True)
    prior_total = jnp.sum(jnp.exp(prior - prior_peak), axis=1, keepdims=True)
    eye = lax.broadcasted_iota(jnp.int32, (P_SIZE, BLK), 0)
    wide = lane_of((P_SIZE, BLK))
    stats = jnp.sum(
        jnp.where(wide == eye + 2 * P_SIZE, prior_peak, 0.0)
        + jnp.where(wide == eye + 3 * P_SIZE, prior_total, 0.0),
        axis=0, keepdims=True,
    )
    stats = jnp.broadcast_to(stats, (S_LOC, BLK))
    peaks = [jnp.max(root_ref[p], axis=1, keepdims=True) for p in range(P_SIZE)]
    for p in range(P_SIZE):
        total = jnp.sum(jnp.exp(root_ref[p] - peaks[p]), axis=1, keepdims=True)
        stats = jnp.where(lanes == p, peaks[p], stats)
        stats = jnp.where(lanes == P_SIZE + p, total, stats)
    stats_ref[...] = stats


def merge(stats):
    is_peak = lane_of((S_LOC, BLK)) % (2 * P_SIZE) < P_SIZE
    peaks = [jnp.where(is_peak, s, pltpu.roll(s, P_SIZE, 1)) for s in stats]
    best = peaks[0]
    for p in peaks[1:]:
        best = jnp.maximum(best, p)
    total = None
    for s, p in zip(stats, peaks):
        term = s * jnp.exp(p - best)
        total = term if total is None else total + term
    return jnp.where(is_peak, best, total)


def merge_kernel(*refs):
    refs[-1][...] = merge([r[...] for r in refs[:-1]])


def place_rows(place_ref, distance, parts, rows):
    return pl.multiple_of(lax.rem(place_ref[1] + distance, parts) * rows, rows)


def shares_kernel(scale, place_ref, map_ref, stats_ref, *refs):
    root_ref, own_sums_ref, other_sums_ref, own_ref, other_ref, weights_ref = refs[:6]
    far, (share_ref, loglik_ref, posterior) = refs[6:8], refs[8:]
    stats = merge([stats_ref[i] for i in range(stats_ref.shape[0])])
    lanes = lane_of((S_LOC, BLK))
    norm = stats + pltpu.roll(jnp.log(stats), BLK - P_SIZE, 1)
    signed = jnp.where(lanes < P_SIZE, norm, 0.0) - jnp.where(
        (lanes >= 2 * P_SIZE) & (lanes < 3 * P_SIZE), norm, 0.0
    )
    loglik = jnp.sum(signed, axis=1, keepdims=True) / (C + P_SIZE)
    loglik_ref[...] = jnp.broadcast_to(loglik, (S_LOC, BLK))
    for p in range(P_SIZE):
        posterior[p] = jnp.exp(root_ref[p] - norm[:, p : p + 1]).astype(jnp.bfloat16)
    rows = far[0].shape[2]
    parts = BLK // rows
    first = place_rows(place_ref, parts // 2, parts, rows)
    turn = lax.rem(BLK - first, BLK)
    for half, (picked_ref, sums_ref) in enumerate(
        ((own_ref, own_sums_ref), (other_ref, other_sums_ref))
    ):
        for k in range(HALF):
            child = child_at(place_ref[0], half, k)
            share = posterior[map_ref[child]].astype(jnp.float32) / sums_ref[k]
            share_ref[half * HALF + k] = share.astype(jnp.bfloat16)
            share = pltpu.roll(share, turn, 1).astype(jnp.bfloat16)[:, :rows]
            picked = jnp.concatenate([picked_ref[k * NZ + z] for z in range(NZ)], axis=1)
            flow = lax.dot_general(
                share, picked, (((0,), (0,)), ((), ())), preferred_element_type=jnp.float32
            )
            for z in range(NZ):
                weight = weights_ref[child, z, pl.ds(first, rows), :].astype(jnp.float32) * scale
                block = flow[:, z * BLK : (z + 1) * BLK] * weight
                far[half][k, z] = block.astype(jnp.bfloat16)


def counts_kernel(scale, place_ref, share_ref, own_ref, other_ref, weights_ref, *refs):
    near, flows = refs[:-1], refs[-1]
    rows = near[0].shape[2]
    parts = BLK // rows
    distances = [d for d in range(parts) if d != parts // 2]
    starts = [place_rows(place_ref, d, parts, rows) for d in distances]
    for half, picked_ref in enumerate((own_ref, other_ref)):
        for k in range(HALF):
            child = child_at(place_ref[0], half, k)
            at = half * HALF + k
            picked = jnp.concatenate([picked_ref[k * NZ + z] for z in range(NZ)], axis=1)
            flows[at % 4] = lax.dot_general(
                share_ref[at], picked, (((0,), (0,)), ((), ())), preferred_element_type=jnp.float32
            )
            for out_ref, start in zip(near, starts):
                flow = flows[at % 4, pl.ds(start, rows), :]
                for z in range(NZ):
                    weight = weights_ref[child, z, pl.ds(start, rows), :].astype(jnp.float32) * scale
                    block = flow[:, z * BLK : (z + 1) * BLK] * weight
                    out_ref[at, z] = block.astype(jnp.bfloat16)


def first_step_kernel(up_ref, down_ref, up_in_ref, down_in_ref, up_out_ref, down_out_ref):
    f32 = jnp.float32
    low, high = pl.ds(0, HALF), pl.ds(HALF, HALF)
    up_out_ref[low] = (up_ref[low].astype(f32) + up_in_ref[...].astype(f32)).astype(jnp.bfloat16)
    up_out_ref[high] = up_ref[high]
    down_out_ref[low] = down_ref[low]
    down_out_ref[high] = (down_ref[high].astype(f32) + down_in_ref[...].astype(f32)).astype(
        jnp.bfloat16
    )


def step_kernel(up_ref, down_ref, up_in_ref, down_in_ref, up_out_ref, down_out_ref):
    f32 = jnp.float32
    up_out_ref[...] = (up_ref[...].astype(f32) + up_in_ref[...].astype(f32)).astype(jnp.bfloat16)
    down_out_ref[...] = (down_ref[...].astype(f32) + down_in_ref[...].astype(f32)).astype(
        jnp.bfloat16
    )


def last_kernel(core_ref, own_ref, up_in_ref, down_in_ref, out_ref):
    f32 = jnp.float32
    core = core_ref[0]
    for half in range(2):
        part = pl.ds(half * HALF, HALF)
        total = own_ref[part].astype(f32) + up_in_ref[part].astype(f32) + down_in_ref[part].astype(f32)
        out_ref[pl.ds(jnp.where(core == half, 0, HALF), HALF)] = total.astype(jnp.bfloat16)


def params(mib):
    return pltpu.CompilerParams(vmem_limit_bytes=mib << 20)


def cost(flops, moved, transcendentals):
    return pl.CostEstimate(flops=flops, bytes_accessed=moved, transcendentals=transcendentals)


def along(a, b):
    pairs = []
    for i in range(32):
        x, y, core = i // 8, i // 2 % 4, i % 2
        dx, dy = (a, b) if core == 0 else (b, a)
        pairs.append((i, (x + dx) % 4 * 8 + (y + dy) % 4 * 2 + core))
    return pairs


SWAP = [(i, i ^ 1) for i in range(32)]


def body(
    child_values,
    parent_values,
    child_logits,
    parent_logits,
    prior_logits,
    weights,
    block_cols,
    parent_map,
):
    f32, bf16, i32 = jnp.float32, jnp.bfloat16, jnp.int32
    shape = jax.ShapeDtypeStruct
    parts = lax.axis_size("batch")
    rows = BLK // parts
    weights = weights[:, 0]
    region = lax.axis_index("region").astype(i32)
    core = lax.rem(region, 2)
    x, y = lax.shift_right_logical(region, 3), lax.shift_right_logical(region, 1) & 3
    place = jnp.stack(
        [
            core,
            lax.axis_index("batch").astype(i32),
            jnp.where(core == 0, x, y),
            jnp.where(core == 0, y, x),
        ]
    )

    columns = block_cols[:, 0].T

    def scores(half):
        return pl.pallas_call(
            child_kernel,
            out_shape=shape((HALF + 1, S_LOC, BLK), bf16),
            in_specs=[SMEM, VMEM, VMEM],
            out_specs=VMEM,
            scratch_shapes=[pltpu.VMEM((HALF, S_LOC, BLK), f32)],
            compiler_params=params(16),
            cost_estimate=cost(1 << 27, 2 << 20, 1 << 20),
            name="child_scores",
        )(half.reshape(1), child_values.T, child_logits)

    given, other_columns = lax.optimization_barrier(
        (lax.ppermute(scores(1 - core), "region", SWAP), lax.ppermute(columns, "region", SWAP))
    )
    kept = scores(core)
    own = pl.pallas_call(
        pack_kernel,
        out_shape=shape((PIECE, S_LOC, BLK), bf16),
        in_specs=[SMEM, VMEM, VMEM],
        out_specs=VMEM,
        compiler_params=params(8),
        name="pack",
    )(place, kept, given)

    def send(value, a, b):
        return lax.ppermute(value, "region", along(a, b))

    parent_in = pl.pallas_call(
        parent_kernel,
        out_shape=shape((P_SIZE, S_LOC, BLK), f32),
        in_specs=[VMEM, VMEM, VMEM],
        out_specs=VMEM,
        compiler_params=params(12),
        cost_estimate=cost(1 << 28, 3 << 20, 1 << 21),
        name="parent_scores",
    )(parent_values.T, parent_logits, prior_logits)
    cut = (PIECE + 1) // 2
    a1, a3 = lax.optimization_barrier((send(own, 1, 0), send(own, -1, 0)))
    c1, c3 = send(a1[:cut], 1, 0), send(a3[cut:], -1, 0)
    near = jnp.concatenate([own, a1])
    near_up, near_down = send(near, 0, 1), send(near, 0, -1)
    c1, c3 = lax.optimization_barrier((c1, c3))
    far = jnp.concatenate([a3, c1, c3])
    far_up, far_down = send(far, 0, 1), send(far, 0, -1)
    near_up, near_down = lax.optimization_barrier((near_up, near_down))
    next_up, next_down = send(near_up[:PIECE], 0, 1), send(near_down[PIECE:], 0, -1)
    far_up, far_down, near_down = lax.optimization_barrier((far_up, far_down, near_down))
    last_up, last_down = send(far_up[:PIECE], 0, 1), send(far_down[PIECE:], 0, -1)
    slots = shape((HALF * NZ + 1, S_LOC, BLK), bf16)
    for_other, pool, powers = pl.pallas_call(
        pick_other_kernel,
        out_shape=(
            slots,
            shape((16 * PIECE, S_LOC, BLK), bf16),
            shape((32, S_LOC, BLK), f32),
        ),
        in_specs=[SMEM, SMEM] + [VMEM] * len(PLACES),
        out_specs=(VMEM, VMEM, VMEM),
        compiler_params=params(22),
        cost_estimate=cost(1 << 22, 20 << 20, 1 << 20),
        name="pick_other",
    )(place, other_columns, near, far, near_up, far_up, near_down, far_down, next_up, next_down, last_up, last_down)
    other = lax.ppermute(for_other, "region", SWAP)
    half_sums = shape((HALF, S_LOC, BLK), f32)
    scores_all = shape((P_SIZE, S_LOC, BLK), f32)
    picked, own_sums, own_root = pl.pallas_call(
        own_sums_kernel,
        out_shape=(shape((HALF * NZ, S_LOC, BLK), bf16), half_sums, scores_all),
        in_specs=[SMEM, SMEM, SMEM] + [VMEM] * 4,
        out_specs=(VMEM,) * 3,
        compiler_params=params(20),
        cost_estimate=cost(1 << 28, 8 << 20, 1 << 19),
        name="own_sums",
    )(place, columns, parent_map, pool, powers, weights, parent_in)
    stats, root, other_sums = pl.pallas_call(
        sums_kernel,
        out_shape=(shape((S_LOC, BLK), f32), scores_all, half_sums),
        in_specs=[SMEM, SMEM] + [VMEM] * 4,
        out_specs=(VMEM,) * 3,
        compiler_params=params(16),
        cost_estimate=cost(1 << 28, 8 << 20, 1 << 20),
        name="row_sums",
    )(place, parent_map, other, weights, own_root, prior_logits)

    def merged(name, *parts_of):
        return pl.pallas_call(
            merge_kernel,
            out_shape=shape((S_LOC, BLK), f32),
            in_specs=[VMEM] * len(parts_of),
            out_specs=VMEM,
            compiler_params=params(4),
            name=name,
        )(*parts_of)

    stats = merged("merge_core", stats, lax.ppermute(stats, "region", SWAP))
    same_core = [[2 * i + c for i in range(16)] for c in range(2)]
    others = [
        lax.all_to_all(
            jnp.broadcast_to(stats[None], (16, S_LOC, BLK)), "region", 0, 0, axis_index_groups=same_core
        )
    ]
    scale = K * NZ * BLK / (S_LOC * parts)
    whole, half_set = shape((C, NZ, rows, BLK), bf16), shape((HALF, NZ, rows, BLK), bf16)
    far_up, far_down, shares, loglik = pl.pallas_call(
        functools.partial(shares_kernel, scale),
        out_shape=(half_set, half_set, shape((C, S_LOC, BLK), bf16), shape((S_LOC, BLK), f32)),
        in_specs=[SMEM, SMEM] + [VMEM] * 7,
        out_specs=(VMEM,) * 4,
        scratch_shapes=[pltpu.VMEM((P_SIZE, S_LOC, BLK), bf16)],
        compiler_params=params(20),
        cost_estimate=cost(1 << 26, 12 << 20, 1 << 19),
        name="shares",
    )(place, parent_map, *others, root, own_sums, other_sums, picked, other, weights)

    def ring(up, down):
        shift = lambda step: [(i, (i + step) % parts) for i in range(parts)]
        return lax.ppermute(up, "batch", shift(1)), lax.ppermute(down, "batch", shift(-1))

    up, down = ring(far_up, far_down)
    n0, n1, n2, n3, n5, n6, n7 = pl.pallas_call(
        functools.partial(counts_kernel, scale),
        out_shape=(whole,) * 7,
        in_specs=[SMEM] + [VMEM] * 4,
        out_specs=(VMEM,) * 7,
        scratch_shapes=[pltpu.VMEM((4, BLK, NZ * BLK), f32)],
        compiler_params=params(20),
        cost_estimate=cost(1 << 20, 1 << 20, 1),
        name="counts",
    )(place, shares, picked, other, weights)
    for kernel, here_up, here_down in (
        (first_step_kernel, n3, n5),
        (step_kernel, n2, n6),
        (step_kernel, n1, n7),
    ):
        up, down = ring(
            *pl.pallas_call(
                kernel,
                out_shape=(whole, whole),
                in_specs=[VMEM] * 4,
                out_specs=(VMEM, VMEM),
                compiler_params=params(8),
                name="ring_add",
            )(here_up, here_down, up, down)
        )
    counts = pl.pallas_call(
        last_kernel,
        out_shape=whole,
        in_specs=[SMEM] + [VMEM] * 3,
        out_specs=VMEM,
        compiler_params=params(8),
        name="ring_last",
    )(place, n0, up, down)
    return (counts[:, None], loglik[:, 0])


def solution(mesh):
    return jax.shard_map(
        body,
        mesh=mesh,
        in_specs=(
            P("batch", None),
            P("batch", None),
            P(None, None, "region"),
            P(None, None, "region"),
            P(None, "region"),
            P(None, "region", None, None, None),
            P(None, "region", None),
            P(),
        ),
        out_specs=(P(None, "region", None, "batch", None), P("batch")),
        check_vma=False,
    )
```

```python
import functools

import jax
import jax.numpy as jnp
from jax import lax
from jax.experimental import pallas as pl
from jax.experimental.pallas import tpu as pltpu
from jax.sharding import PartitionSpec as P

K = 4096
BLK = 128
NZ = 4
C = 32
P_SIZE = 32
S_LOC = 64
LN2 = 0.6931471805599453
LOG2E = 1.4426950408889634
HALF = C // 2
PIECE = 2 * HALF + 1
VMEM = pl.BlockSpec(memory_space=pltpu.VMEM)
SMEM = pl.BlockSpec(memory_space=pltpu.SMEM)
HBM = pl.BlockSpec(memory_space=pltpu.HBM)


def lane_of(shape):
    return lax.broadcasted_iota(jnp.int32, shape, len(shape) - 1)


def look_up(values, table):
    wide = table.astype(jnp.float32)
    top = jnp.max(wide, axis=0, keepdims=True)
    log_norm = jnp.log(jnp.sum(jnp.exp(wide - top), axis=0, keepdims=True)) + top
    hot = (values == lane_of((S_LOC, table.shape[0]))).astype(jnp.float32)
    looked = jnp.dot(hot.astype(jnp.bfloat16), table, preferred_element_type=jnp.float32)
    return looked - log_norm


def child_scores(half, values, table_of, out_ref, inputs):
    values = values.T
    values = jnp.where(half == 0, values[:, :HALF], values[:, HALF:])
    for k in range(HALF):
        inputs[k] = look_up(values[:, k : k + 1], table_of(k))
    powers = jnp.zeros((S_LOC, BLK), jnp.float32)
    lanes = lane_of((S_LOC, BLK))
    for k in range(HALF):
        powers = jnp.where(lanes == k, jnp.max(inputs[k], axis=1, keepdims=True), powers)
    powers = jnp.ceil(powers * LOG2E).astype(jnp.bfloat16)
    out_ref[HALF] = powers
    powers = powers.astype(jnp.float32) * LN2
    for k in range(HALF):
        out_ref[k] = jnp.exp(inputs[k] - powers[:, k : k + 1]).astype(jnp.bfloat16)


def child_kernel(half_ref, values_ref, table_ref, out_ref, inputs):
    half = half_ref[0]
    child_scores(half, values_ref[...], lambda k: table_ref[half * HALF + k], out_ref, inputs)


def first_child_kernel(half_ref, values_ref, table_ref, out_ref, inputs, values, table, sems):
    half = half_ref[0]
    chunks = sems.shape[0] - 1
    size = HALF // chunks
    copies = [pltpu.make_async_copy(values_ref, values, sems.at[chunks])]
    for n in range(chunks):
        source = table_ref.at[pl.ds(half * HALF + n * size, size)]
        copies.append(pltpu.make_async_copy(source, table.at[pl.ds(n * size, size)], sems.at[n]))
    for copy in copies:
        copy.start()
    copies[0].wait()

    def table_of(k):
        if k % size == 0:
            copies[1 + k // size].wait()
        return table[k]

    child_scores(half, values[...], table_of, out_ref, inputs)


def pack_kernel(core_ref, own_ref, other_ref, out_ref):
    core = core_ref[0]
    out_ref[pl.ds(core * HALF, HALF)] = own_ref[:HALF]
    out_ref[pl.ds((1 - core) * HALF, HALF)] = other_ref[:HALF]
    own = own_ref[HALF].astype(jnp.float32)
    other = other_ref[HALF].astype(jnp.float32)
    low = jnp.where(core == 0, own, other)
    high = jnp.where(core == 0, other, own)
    powers = jnp.where(lane_of((S_LOC, BLK)) < HALF, low, pltpu.roll(high, HALF, 1))
    out_ref[2 * HALF] = powers.astype(jnp.bfloat16)


def parent_kernel(values_ref, table_ref, prior_ref, out_ref):
    values = values_ref[...].T
    for p in range(P_SIZE):
        out_ref[p] = look_up(values[:, p : p + 1], table_ref[p]) + prior_ref[p : p + 1, :]


PLACES = (
    ((0, 0), (3, 0)),
    ((1, 0), (2, 0)),
    ((0, 3), (3, 3)),
    ((1, 3), (2, 3)),
    ((0, 1), (3, 1)),
    ((1, 1), (2, 1)),
    ((0, 2),),
    ((3, 2),),
    ((1, 2),),
    ((2, 2),),
)


def codes_of(place_ref, columns_ref, k):
    core = place_ref[0]
    codes = []
    for z in range(NZ):
        column = columns_ref[z, core * HALF + k]
        x, y = lax.shift_right_logical(column, 3), lax.shift_right_logical(column, 1) & 3
        a = (jnp.where(core == 0, x, y) - place_ref[2]) & 3
        b = (jnp.where(core == 0, y, x) - place_ref[3]) & 3
        codes.append((a * 4 + b) * 2 + (column & 1))
    return codes


def pick_child(codes, k, pool, powers):
    power = [powers[code][:, k : k + 1] for code in codes]
    top = jnp.maximum(jnp.maximum(power[0], power[1]), jnp.maximum(power[2], power[3]))
    blocks = []
    for code, mine in zip(codes, power):
        factor = jnp.broadcast_to(jnp.exp2(mine - top), (S_LOC, BLK))
        block = pool[lax.shift_right_logical(code, 1) * PIECE + (code & 1) * HALF + k]
        blocks.append((block.astype(jnp.float32) * factor).astype(jnp.bfloat16))
    return blocks, top


def pick_other_kernel(place_ref, columns_ref, *refs):
    sources, (out_ref, pool, powers) = refs[: len(PLACES)], refs[len(PLACES) :]

    def collect(k, carry):
        for source, places in zip(sources, PLACES):
            for n, (a, b) in enumerate(places):
                pool[(a * 4 + b) * PIECE + k] = source[n * PIECE + k]
        return carry

    lax.fori_loop(0, PIECE, collect, 0)
    for piece in range(16):
        both = pool[piece * PIECE + 2 * HALF].astype(jnp.float32)
        powers[2 * piece] = both
        powers[2 * piece + 1] = pltpu.roll(both, BLK - HALF, 1)
    lanes = lane_of((S_LOC, BLK))
    tops = jnp.zeros((S_LOC, BLK), jnp.float32)
    for k in range(HALF):
        blocks, top = pick_child(codes_of(place_ref, columns_ref, k), k, pool, powers)
        tops = jnp.where(lanes == k, top, tops)
        for z in range(NZ):
            out_ref[k * NZ + z] = blocks[z]
    out_ref[HALF * NZ] = tops.astype(jnp.bfloat16)


def row_sum(blocks, weights_ref, child):
    total = None
    for z in range(0, NZ, 2):
        picked = jnp.concatenate(blocks[z : z + 2], axis=1)
        wide = jnp.concatenate([weights_ref[child, z], weights_ref[child, z + 1]], axis=1)
        term = lax.dot_general(
            picked, wide, (((1,), (1,)), ((), ())), preferred_element_type=jnp.float32
        )
        total = term if total is None else total + term
    return total


def child_at(core, half, k):
    return jnp.where(core == half, k, HALF + k)


def own_sums_kernel(
    place_ref, columns_ref, map_ref, pool, powers, weights_ref, parent_ref,
    out_ref, sums_ref, root_ref,
):
    root_ref[...] = parent_ref[...]
    for k in range(HALF):
        child = child_at(place_ref[0], 0, k)
        blocks, top = pick_child(codes_of(place_ref, columns_ref, k), k, pool, powers)
        for z in range(NZ):
            out_ref[k * NZ + z] = blocks[z]
        row_sums = row_sum(blocks, weights_ref, child)
        sums_ref[k] = row_sums
        owner = map_ref[child]
        root_ref[owner] = root_ref[owner] + (jnp.log(row_sums) + top * LN2)


def sums_kernel(
    place_ref, map_ref, other_ref, weights_ref, own_root_ref, prior_ref,
    stats_ref, root_ref, sums_ref,
):
    root_ref[...] = own_root_ref[...]
    tops = other_ref[HALF * NZ].astype(jnp.float32) * LN2
    for k in range(HALF):
        child = child_at(place_ref[0], 1, k)
        row_sums = row_sum([other_ref[k * NZ + z] for z in range(NZ)], weights_ref, child)
        sums_ref[k] = row_sums
        owner = map_ref[child]
        root_ref[owner] = root_ref[owner] + (jnp.log(row_sums) + tops[:, k : k + 1])
    lanes = lane_of((S_LOC, BLK))
    prior = prior_ref[...]
    prior_peak = jnp.max(prior, axis=1, keepdims=True)
    prior_total = jnp.sum(jnp.exp(prior - prior_peak), axis=1, keepdims=True)
    eye = lax.broadcasted_iota(jnp.int32, (P_SIZE, BLK), 0)
    wide = lane_of((P_SIZE, BLK))
    stats = jnp.sum(
        jnp.where(wide == eye + 2 * P_SIZE, prior_peak, 0.0)
        + jnp.where(wide == eye + 3 * P_SIZE, prior_total, 0.0),
        axis=0, keepdims=True,
    )
    stats = jnp.broadcast_to(stats, (S_LOC, BLK))
    peaks = [jnp.max(root_ref[p], axis=1, keepdims=True) for p in range(P_SIZE)]
    for p in range(P_SIZE):
        total = jnp.sum(jnp.exp(root_ref[p] - peaks[p]), axis=1, keepdims=True)
        stats = jnp.where(lanes == p, peaks[p], stats)
        stats = jnp.where(lanes == P_SIZE + p, total, stats)
    stats_ref[...] = stats


def merge(stats):
    is_peak = lane_of((S_LOC, BLK)) % (2 * P_SIZE) < P_SIZE
    peaks = [jnp.where(is_peak, s, pltpu.roll(s, P_SIZE, 1)) for s in stats]
    best = peaks[0]
    for p in peaks[1:]:
        best = jnp.maximum(best, p)
    total = None
    for s, p in zip(stats, peaks):
        term = s * jnp.exp(p - best)
        total = term if total is None else total + term
    return jnp.where(is_peak, best, total)


def merge_kernel(*refs):
    refs[-1][...] = merge([r[...] for r in refs[:-1]])


def place_rows(place_ref, distance, parts, rows):
    return pl.multiple_of(lax.rem(place_ref[1] + distance, parts) * rows, rows)


def shares_kernel(scale, place_ref, map_ref, stats_ref, *refs):
    root_ref, own_sums_ref, other_sums_ref, own_ref, other_ref, weights_ref = refs[:6]
    far, (share_ref, loglik_ref, posterior) = refs[6:8], refs[8:]
    stats = merge([stats_ref[i] for i in range(stats_ref.shape[0])])
    lanes = lane_of((S_LOC, BLK))
    norm = stats + pltpu.roll(jnp.log(stats), BLK - P_SIZE, 1)
    signed = jnp.where(lanes < P_SIZE, norm, 0.0) - jnp.where(
        (lanes >= 2 * P_SIZE) & (lanes < 3 * P_SIZE), norm, 0.0
    )
    loglik = jnp.sum(signed, axis=1, keepdims=True) / (C + P_SIZE)
    loglik_ref[...] = jnp.broadcast_to(loglik, (S_LOC, BLK))
    for p in range(P_SIZE):
        posterior[p] = jnp.exp(root_ref[p] - norm[:, p : p + 1]).astype(jnp.bfloat16)
    rows = far[0].shape[2]
    parts = BLK // rows
    first = place_rows(place_ref, parts // 2, parts, rows)
    turn = lax.rem(BLK - first, BLK)
    for half, (picked_ref, sums_ref) in enumerate(
        ((own_ref, own_sums_ref), (other_ref, other_sums_ref))
    ):
        for k in range(HALF):
            child = child_at(place_ref[0], half, k)
            share = posterior[map_ref[child]].astype(jnp.float32) / sums_ref[k]
            share_ref[half * HALF + k] = share.astype(jnp.bfloat16)
            share = pltpu.roll(share, turn, 1).astype(jnp.bfloat16)[:, :rows]
            picked = jnp.concatenate([picked_ref[k * NZ + z] for z in range(NZ)], axis=1)
            flow = lax.dot_general(
                share, picked, (((0,), (0,)), ((), ())), preferred_element_type=jnp.float32
            )
            for z in range(NZ):
                weight = weights_ref[child, z, pl.ds(first, rows), :].astype(jnp.float32) * scale
                block = flow[:, z * BLK : (z + 1) * BLK] * weight
                far[half][k, z] = block.astype(jnp.bfloat16)


def counts_kernel(scale, place_ref, share_ref, own_ref, other_ref, weights_ref, *refs):
    near, flows = refs[:-1], refs[-1]
    rows = near[0].shape[2]
    parts = BLK // rows
    distances = [d for d in range(parts) if d != parts // 2]
    starts = [place_rows(place_ref, d, parts, rows) for d in distances]
    for half, picked_ref in enumerate((own_ref, other_ref)):
        for k in range(HALF):
            child = child_at(place_ref[0], half, k)
            at = half * HALF + k
            picked = jnp.concatenate([picked_ref[k * NZ + z] for z in range(NZ)], axis=1)
            flows[at % 4] = lax.dot_general(
                share_ref[at], picked, (((0,), (0,)), ((), ())), preferred_element_type=jnp.float32
            )
            for out_ref, start in zip(near, starts):
                flow = flows[at % 4, pl.ds(start, rows), :]
                for z in range(NZ):
                    weight = weights_ref[child, z, pl.ds(start, rows), :].astype(jnp.float32) * scale
                    block = flow[:, z * BLK : (z + 1) * BLK] * weight
                    out_ref[at, z] = block.astype(jnp.bfloat16)


def first_step_kernel(up_ref, down_ref, up_in_ref, down_in_ref, up_out_ref, down_out_ref):
    f32 = jnp.float32
    low, high = pl.ds(0, HALF), pl.ds(HALF, HALF)
    up_out_ref[low] = (up_ref[low].astype(f32) + up_in_ref[...].astype(f32)).astype(jnp.bfloat16)
    up_out_ref[high] = up_ref[high]
    down_out_ref[low] = down_ref[low]
    down_out_ref[high] = (down_ref[high].astype(f32) + down_in_ref[...].astype(f32)).astype(
        jnp.bfloat16
    )


def step_kernel(up_ref, down_ref, up_in_ref, down_in_ref, up_out_ref, down_out_ref):
    f32 = jnp.float32
    up_out_ref[...] = (up_ref[...].astype(f32) + up_in_ref[...].astype(f32)).astype(jnp.bfloat16)
    down_out_ref[...] = (down_ref[...].astype(f32) + down_in_ref[...].astype(f32)).astype(
        jnp.bfloat16
    )


def last_kernel(core_ref, own_ref, up_in_ref, down_in_ref, out_ref):
    f32 = jnp.float32
    core = core_ref[0]
    for half in range(2):
        part = pl.ds(half * HALF, HALF)
        total = own_ref[part].astype(f32) + up_in_ref[part].astype(f32) + down_in_ref[part].astype(f32)
        out_ref[pl.ds(jnp.where(core == half, 0, HALF), HALF)] = total.astype(jnp.bfloat16)


def params(mib):
    return pltpu.CompilerParams(vmem_limit_bytes=mib << 20)


def cost(flops, moved, transcendentals):
    return pl.CostEstimate(flops=flops, bytes_accessed=moved, transcendentals=transcendentals)


def along(a, b):
    pairs = []
    for i in range(32):
        x, y, core = i // 8, i // 2 % 4, i % 2
        dx, dy = (a, b) if core == 0 else (b, a)
        pairs.append((i, (x + dx) % 4 * 8 + (y + dy) % 4 * 2 + core))
    return pairs


SWAP = [(i, i ^ 1) for i in range(32)]


def body(
    child_values,
    parent_values,
    child_logits,
    parent_logits,
    prior_logits,
    weights,
    block_cols,
    parent_map,
):
    f32, bf16, i32 = jnp.float32, jnp.bfloat16, jnp.int32
    shape = jax.ShapeDtypeStruct
    parts = lax.axis_size("batch")
    rows = BLK // parts
    weights = weights[:, 0]
    region = lax.axis_index("region").astype(i32)
    core = lax.rem(region, 2)
    x, y = lax.shift_right_logical(region, 3), lax.shift_right_logical(region, 1) & 3
    place = jnp.stack(
        [
            core,
            lax.axis_index("batch").astype(i32),
            jnp.where(core == 0, x, y),
            jnp.where(core == 0, y, x),
        ]
    )

    columns = block_cols[:, 0].T

    def scores(kernel, half, in_space, more_scratch, mib):
        return pl.pallas_call(
            kernel,
            out_shape=shape((HALF + 1, S_LOC, BLK), bf16),
            in_specs=[SMEM, in_space, in_space],
            out_specs=VMEM,
            scratch_shapes=[pltpu.VMEM((HALF, S_LOC, BLK), f32)] + more_scratch,
            compiler_params=params(mib),
            cost_estimate=cost(1 << 27, 2 << 20, 1 << 20),
            name="child_scores",
        )(half.reshape(1), child_values.T, child_logits)

    fetched = [
        pltpu.VMEM((C, S_LOC), i32),
        pltpu.VMEM((HALF,) + child_logits.shape[1:], bf16),
        pltpu.SemaphoreType.DMA((5,)),
    ]
    given = scores(first_child_kernel, 1 - core, HBM, fetched, 56)
    given, other_columns = lax.optimization_barrier(
        (lax.ppermute(given, "region", SWAP), lax.ppermute(columns, "region", SWAP))
    )
    kept = scores(child_kernel, core, VMEM, [], 16)
    own = pl.pallas_call(
        pack_kernel,
        out_shape=shape((PIECE, S_LOC, BLK), bf16),
        in_specs=[SMEM, VMEM, VMEM],
        out_specs=VMEM,
        compiler_params=params(8),
        name="pack",
    )(place, kept, given)

    def send(value, a, b):
        return lax.ppermute(value, "region", along(a, b))

    parent_in = pl.pallas_call(
        parent_kernel,
        out_shape=shape((P_SIZE, S_LOC, BLK), f32),
        in_specs=[VMEM, VMEM, VMEM],
        out_specs=VMEM,
        compiler_params=params(12),
        cost_estimate=cost(1 << 28, 3 << 20, 1 << 21),
        name="parent_scores",
    )(parent_values.T, parent_logits, prior_logits)
    cut = (PIECE + 1) // 2
    a1, a3 = lax.optimization_barrier((send(own, 1, 0), send(own, -1, 0)))
    c1, c3 = send(a1[:cut], 1, 0), send(a3[cut:], -1, 0)
    near = jnp.concatenate([own, a1])
    near_up, near_down = send(near, 0, 1), send(near, 0, -1)
    c1, c3 = lax.optimization_barrier((c1, c3))
    far = jnp.concatenate([a3, c1, c3])
    far_up, far_down = send(far, 0, 1), send(far, 0, -1)
    near_up, near_down = lax.optimization_barrier((near_up, near_down))
    next_up, next_down = send(near_up[:PIECE], 0, 1), send(near_down[PIECE:], 0, -1)
    far_up, far_down, near_down = lax.optimization_barrier((far_up, far_down, near_down))
    last_up, last_down = send(far_up[:PIECE], 0, 1), send(far_down[PIECE:], 0, -1)
    slots = shape((HALF * NZ + 1, S_LOC, BLK), bf16)
    for_other, pool, powers = pl.pallas_call(
        pick_other_kernel,
        out_shape=(
            slots,
            shape((16 * PIECE, S_LOC, BLK), bf16),
            shape((32, S_LOC, BLK), f32),
        ),
        in_specs=[SMEM, SMEM] + [VMEM] * len(PLACES),
        out_specs=(VMEM, VMEM, VMEM),
        compiler_params=params(22),
        cost_estimate=cost(1 << 22, 20 << 20, 1 << 20),
        name="pick_other",
    )(place, other_columns, near, far, near_up, far_up, near_down, far_down, next_up, next_down, last_up, last_down)
    other = lax.ppermute(for_other, "region", SWAP)
    half_sums = shape((HALF, S_LOC, BLK), f32)
    scores_all = shape((P_SIZE, S_LOC, BLK), f32)
    picked, own_sums, own_root = pl.pallas_call(
        own_sums_kernel,
        out_shape=(shape((HALF * NZ, S_LOC, BLK), bf16), half_sums, scores_all),
        in_specs=[SMEM, SMEM, SMEM] + [VMEM] * 4,
        out_specs=(VMEM,) * 3,
        compiler_params=params(20),
        cost_estimate=cost(1 << 28, 8 << 20, 1 << 19),
        name="own_sums",
    )(place, columns, parent_map, pool, powers, weights, parent_in)
    stats, root, other_sums = pl.pallas_call(
        sums_kernel,
        out_shape=(shape((S_LOC, BLK), f32), scores_all, half_sums),
        in_specs=[SMEM, SMEM] + [VMEM] * 4,
        out_specs=(VMEM,) * 3,
        compiler_params=params(16),
        cost_estimate=cost(1 << 28, 8 << 20, 1 << 20),
        name="row_sums",
    )(place, parent_map, other, weights, own_root, prior_logits)

    def merged(name, *parts_of):
        return pl.pallas_call(
            merge_kernel,
            out_shape=shape((S_LOC, BLK), f32),
            in_specs=[VMEM] * len(parts_of),
            out_specs=VMEM,
            compiler_params=params(4),
            name=name,
        )(*parts_of)

    stats = merged("merge_core", stats, lax.ppermute(stats, "region", SWAP))
    same_core = [[2 * i + c for i in range(16)] for c in range(2)]
    others = [
        lax.all_to_all(
            jnp.broadcast_to(stats[None], (16, S_LOC, BLK)), "region", 0, 0, axis_index_groups=same_core
        )
    ]
    scale = K * NZ * BLK / (S_LOC * parts)
    whole, half_set = shape((C, NZ, rows, BLK), bf16), shape((HALF, NZ, rows, BLK), bf16)
    far_up, far_down, shares, loglik = pl.pallas_call(
        functools.partial(shares_kernel, scale),
        out_shape=(half_set, half_set, shape((C, S_LOC, BLK), bf16), shape((S_LOC, BLK), f32)),
        in_specs=[SMEM, SMEM] + [VMEM] * 7,
        out_specs=(VMEM,) * 4,
        scratch_shapes=[pltpu.VMEM((P_SIZE, S_LOC, BLK), bf16)],
        compiler_params=params(20),
        cost_estimate=cost(1 << 26, 12 << 20, 1 << 19),
        name="shares",
    )(place, parent_map, *others, root, own_sums, other_sums, picked, other, weights)

    def ring(up, down):
        shift = lambda step: [(i, (i + step) % parts) for i in range(parts)]
        return lax.ppermute(up, "batch", shift(1)), lax.ppermute(down, "batch", shift(-1))

    up, down = ring(far_up, far_down)
    n0, n1, n2, n3, n5, n6, n7 = pl.pallas_call(
        functools.partial(counts_kernel, scale),
        out_shape=(whole,) * 7,
        in_specs=[SMEM] + [VMEM] * 4,
        out_specs=(VMEM,) * 7,
        scratch_shapes=[pltpu.VMEM((4, BLK, NZ * BLK), f32)],
        compiler_params=params(20),
        cost_estimate=cost(1 << 20, 1 << 20, 1),
        name="counts",
    )(place, shares, picked, other, weights)
    for kernel, here_up, here_down in (
        (first_step_kernel, n3, n5),
        (step_kernel, n2, n6),
        (step_kernel, n1, n7),
    ):
        up, down = ring(
            *pl.pallas_call(
                kernel,
                out_shape=(whole, whole),
                in_specs=[VMEM] * 4,
                out_specs=(VMEM, VMEM),
                compiler_params=params(8),
                name="ring_add",
            )(here_up, here_down, up, down)
        )
    counts = pl.pallas_call(
        last_kernel,
        out_shape=whole,
        in_specs=[SMEM] + [VMEM] * 3,
        out_specs=VMEM,
        compiler_params=params(8),
        name="ring_last",
    )(place, n0, up, down)
    return (counts[:, None], loglik[:, 0])


def solution(mesh):
    return jax.shard_map(
        body,
        mesh=mesh,
        in_specs=(
            P("batch", None),
            P("batch", None),
            P(None, None, "region"),
            P(None, None, "region"),
            P(None, "region"),
            P(None, "region", None, None, None),
            P(None, "region", None),
            P(),
        ),
        out_specs=(P(None, "region", None, "batch", None), P("batch")),
        check_vma=False,
    )
```
